128 devices in a mesh: dp: 16 (over y_lo, x, core), tensor: 8 (over y_hi, z).
Axes of the slice: x: 4, y: 4 (y_hi: 2, y_lo: 2; y = y_hi * 2 + y_lo), z: 4, core: 2. Of those that a mesh axis runs over, the one named last changes fastest.
Arguments:
- block_input: bfloat16 [16384, 2560], P(('dp', 'tensor')), may hold values from -6 to 6
- out_grad: bfloat16 [16384, 2560], P(('dp', 'tensor')), may hold values from -6 to 6
- norm_gains: float32 [6144], P(('dp', 'tensor')), may hold values from 0.5 to 1.5
- latent_weight: float32 [2560, 1056], P(('dp', 'tensor')), may hold values from -0.125 to 0.125
- query_weight: float32 [768, 3840], P('dp', 'tensor'), may hold values from -0.21875 to 0.21875
- keys_weight: float32 [256, 5120], P('dp', 'tensor'), may hold values from -0.375 to 0.375
- output_weight: float32 [2560, 2560], P('tensor', 'dp'), may hold values from -2 to 2
- gate_weight: float32 [2560, 6400], P('dp', 'tensor'), may hold values from -0.125 to 0.125
- up_weight: float32 [2560, 6400], P('dp', 'tensor'), may hold values from -0.125 to 0.125
- down_weight: float32 [6400, 2560], P('tensor', 'dp'), may hold values from -0.625 to 0.625
- gains_moment: float32 [6144], P(('dp', 'tensor')), may hold values from -48 to 48
- gains_second: float32 [6144], P(('dp', 'tensor')), may hold values from 294.912 to 1179.648
- latent_moment: float32 [2560, 1056], P(('dp', 'tensor')), may hold values from -32 to 32
- latent_second: float32 [2560, 1056], P(('dp', 'tensor')), may hold values from 131.072 to 524.288
- query_moment: float32 [768, 3840], P('dp', 'tensor'), may hold values from -16 to 16
- query_second: float32 [768, 3840], P('dp', 'tensor'), may hold values from 32.768 to 131.072
- keys_moment: float32 [256, 5120], P('dp', 'tensor'), may hold values from -40 to 40
- keys_second: float32 [256, 5120], P('dp', 'tensor'), may hold values from 204.8 to 819.2
- output_moment: float32 [2560, 2560], P('tensor', 'dp'), may hold values from -3.5 to 3.5
- output_second: float32 [2560, 2560], P('tensor', 'dp'), may hold values from 1.441792 to 5.7344
- gate_moment: float32 [2560, 6400], P('dp', 'tensor'), may hold values from -48 to 48
- gate_second: float32 [2560, 6400], P('dp', 'tensor'), may hold values from 245.76 to 983.04
- up_moment: float32 [2560, 6400], P('dp', 'tensor'), may hold values from -48 to 48
- up_second: float32 [2560, 6400], P('dp', 'tensor'), may hold values from 245.76 to 983.04
- down_moment: float32 [6400, 2560], P('tensor', 'dp'), may hold values from -8 to 8
- down_second: float32 [6400, 2560], P('tensor', 'dp'), may hold values from 9.33888 to 37.6832
Outputs:
- block_output: float32 [16384, 2560], P(('dp', 'tensor'))
- input_grad: float32 [16384, 2560], P(('dp', 'tensor'))
- next_gains: float32 [6144], P(('dp', 'tensor'))
- moment_gains: float32 [6144], P(('dp', 'tensor'))
- second_gains: float32 [6144], P(('dp', 'tensor'))
- next_latent: float32 [2560, 1056], P(('dp', 'tensor'))
- moment_latent: float32 [2560, 1056], P(('dp', 'tensor'))
- second_latent: float32 [2560, 1056], P(('dp', 'tensor'))
- next_query: float32 [768, 3840], P('dp', 'tensor')
- moment_query: float32 [768, 3840], P('dp', 'tensor')
- second_query: float32 [768, 3840], P('dp', 'tensor')
- next_keys: float32 [256, 5120], P('dp', 'tensor')
- moment_keys: float32 [256, 5120], P('dp', 'tensor')
- second_keys: float32 [256, 5120], P('dp', 'tensor')
- next_output: float32 [2560, 2560], P('tensor', 'dp')
- moment_output: float32 [2560, 2560], P('tensor', 'dp')
- second_output: float32 [2560, 2560], P('tensor', 'dp')
- next_gate: float32 [2560, 6400], P('dp', 'tensor')
- moment_gate: float32 [2560, 6400], P('dp', 'tensor')
- second_gate: float32 [2560, 6400], P('dp', 'tensor')
- next_up: float32 [2560, 6400], P('dp', 'tensor')
- moment_up: float32 [2560, 6400], P('dp', 'tensor')
- second_up: float32 [2560, 6400], P('dp', 'tensor')
- next_down: float32 [6400, 2560], P('tensor', 'dp')
- moment_down: float32 [6400, 2560], P('tensor', 'dp')
- second_down: float32 [6400, 2560], P('tensor', 'dp')
The draws below stay inside these ranges and needn't reach their ends.
All inputs are finite; a program needn't handle non-finite values.
Results may differ from the reference program's by a relative error of at most 0.035.
Values may be sent and summed in bfloat16 or wider, within the bound.
No kernel may reach another device: no remote copies, remote signals or barrier semaphores. Data moves between devices by JAX's collectives and lax.ppermute only.
A program may use at most 192 MiB of HBM per device.

```python
import math
import jax
import jax.numpy as jnp
from jax import lax

D = 2560
HEADS = 40
NOPE = 64
ROPE = 32
VDIM = 64
QR = 768
KVR = 256
FF = 6400
SEQ = 1024
STEP = 10
TOKENS = 16384
N_DP = 16


def shard_levels(own_key, extent, cuts, smallest, top_value):
    level, own = 1.0, jax.random.fold_in(own_key, 6)
    for position, blocks in cuts:
        steps = jnp.exp(jax.random.uniform(jax.random.fold_in(own, position), (blocks,), jnp.float32, smallest / len(cuts), top_value / len(cuts)))
        level = level * jnp.repeat(steps, extent[position] // blocks).reshape([-1 if axis == position else 1 for axis in range(len(extent))])
    return level


def noise(stream_key, extent, width, limit, shards=(), kind=jnp.bfloat16):
    array = width * jax.random.normal(stream_key, extent, jnp.float32)
    if shards:
        array = array * shard_levels(stream_key, extent, shards, -0.22, 0.18)
    return jnp.clip(array, -limit, limit).astype(kind)


def setup_inputs(seed: int = 0) -> dict:
    splits = jax.random.split(jax.random.key(seed), 27)
    return {
        "block_input": noise(splits[0], (TOKENS, D), 1.0, 6.0, ((0, 128),)),
        "out_grad": noise(splits[1], (TOKENS, D), 1.0, 6.0, ((0, 128),)),
        "norm_gains": jnp.clip(1.0 + 0.1 * jax.random.normal(splits[2], (2 * D + QR + KVR,), jnp.float32), 0.5, 1.5),
        "latent_weight": noise(splits[3], (D, QR + KVR + ROPE), D ** -0.5, 0.125, ((0, 128),), jnp.float32),
        "query_weight": noise(splits[4], (QR, HEADS * (NOPE + ROPE)), QR ** -0.5, 0.21875, ((0, 16), (1, 8)), jnp.float32),
        "keys_weight": noise(splits[5], (KVR, HEADS * (NOPE + VDIM)), KVR ** -0.5, 0.375, ((0, 16), (1, 8)), jnp.float32),
        "output_weight": noise(splits[6], (HEADS * VDIM, D), (HEADS * VDIM // 256) ** -0.5, 2.0, ((0, 8), (1, 16)), jnp.float32),
        "gate_weight": noise(splits[7], (D, FF), D ** -0.5, 0.125, ((0, 16), (1, 8)), jnp.float32),
        "up_weight": noise(splits[8], (D, FF), D ** -0.5, 0.125, ((0, 16), (1, 8)), jnp.float32),
        "down_weight": noise(splits[9], (FF, D), (FF // 64) ** -0.5, 0.625, ((0, 8), (1, 16)), jnp.float32),
        "gains_moment": noise(splits[10], (2 * D + QR + KVR,), (0.066 * TOKENS ** 0.5), 48.0, ((0, 128),), jnp.float32),
        "gains_second": jnp.clip(jnp.exp(math.log(1179.648) - 1.3862944 * jax.random.uniform(splits[11], (2 * D + QR + KVR,), jnp.float32) ** shard_levels(splits[11], (2 * D + QR + KVR,), ((0, 128),), -0.2, 0.2)), 294.912, 1179.648),
        "latent_moment": noise(splits[12], (D, QR + KVR + ROPE), (0.044 * TOKENS ** 0.5), 32.0, ((0, 128),), jnp.float32),
        "latent_second": jnp.clip(jnp.exp(math.log(524.288) - 1.3862944 * jax.random.uniform(splits[13], (D, QR + KVR + ROPE), jnp.float32) ** shard_levels(splits[13], (D, QR + KVR + ROPE), ((0, 128),), -0.2, 0.2)), 131.072, 524.288),
        "query_moment": noise(splits[14], (QR, HEADS * (NOPE + ROPE)), (0.022 * TOKENS ** 0.5), 16.0, ((0, 16), (1, 8)), jnp.float32),
        "query_second": jnp.clip(jnp.exp(math.log(131.072) - 1.3862944 * jax.random.uniform(splits[15], (QR, HEADS * (NOPE + ROPE)), jnp.float32) ** shard_levels(splits[15], (QR, HEADS * (NOPE + ROPE)), ((0, 16), (1, 8)), -0.2, 0.2)), 32.768, 131.072),
        "keys_moment": noise(splits[16], (KVR, HEADS * (NOPE + VDIM)), (0.055 * TOKENS ** 0.5), 40.0, ((0, 16), (1, 8)), jnp.float32),
        "keys_second": jnp.clip(jnp.exp(math.log(819.2) - 1.3862944 * jax.random.uniform(splits[17], (KVR, HEADS * (NOPE + VDIM)), jnp.float32) ** shard_levels(splits[17], (KVR, HEADS * (NOPE + VDIM)), ((0, 16), (1, 8)), -0.2, 0.2)), 204.8, 819.2),
        "output_moment": noise(splits[18], (HEADS * VDIM, D), (0.0046 * TOKENS ** 0.5), 3.5, ((0, 8), (1, 16)), jnp.float32),
        "output_second": jnp.clip(jnp.exp(math.log(5.7344) - 1.3805963 * jax.random.uniform(splits[19], (HEADS * VDIM, D), jnp.float32) ** shard_levels(splits[19], (HEADS * VDIM, D), ((0, 8), (1, 16)), -0.2, 0.2)), 1.441792, 5.7344),
        "gate_moment": noise(splits[20], (D, FF), (0.06 * TOKENS ** 0.5), 48.0, ((0, 16), (1, 8)), jnp.float32),
        "gate_second": jnp.clip(jnp.exp(math.log(983.04) - 1.3862944 * jax.random.uniform(splits[21], (D, FF), jnp.float32) ** shard_levels(splits[21], (D, FF), ((0, 16), (1, 8)), -0.2, 0.2)), 245.76, 983.04),
        "up_moment": noise(splits[22], (D, FF), (0.06 * TOKENS ** 0.5), 48.0, ((0, 16), (1, 8)), jnp.float32),
        "up_second": jnp.clip(jnp.exp(math.log(983.04) - 1.3862944 * jax.random.uniform(splits[23], (D, FF), jnp.float32) ** shard_levels(splits[23], (D, FF), ((0, 16), (1, 8)), -0.2, 0.2)), 245.76, 983.04),
        "down_moment": noise(splits[24], (FF, D), (0.0118 * TOKENS ** 0.5), 8.0, ((0, 8), (1, 16)), jnp.float32),
        "down_second": jnp.clip(jnp.exp(math.log(37.6832) - 1.3950281 * jax.random.uniform(splits[25], (FF, D), jnp.float32) ** shard_levels(splits[25], (FF, D), ((0, 8), (1, 16)), -0.2, 0.2)), 9.33888, 37.6832),
    }


EPS = 1e-05
RESIDUAL = 1.4 / math.sqrt(62.0)
BETA_ONE = 0.9
BETA_TWO = 0.95
ADAM_EPS = 1e-08
HIGH = lax.Precision.HIGHEST

@jax.custom_vjp
def low(v):
    return lax.optimization_barrier(v.astype(jnp.bfloat16)).astype(jnp.float32)

@jax.custom_vjp
def low_back(v):
    return v

def low_keep(v):
    return (low(v), None)

def low_pass(kept, grad):
    return (grad,)

def back_keep(v):
    return (v, None)

def back_low(kept, grad):
    return (low(grad),)
low.defvjp(low_keep, low_pass)
low_back.defvjp(back_keep, back_low)

def rotate(values, cosine, sine):
    half = values.shape[-1] // 2
    first = values[..., :half]
    second = values[..., half:]
    return jnp.concatenate([first * cosine - second * sine, second * cosine + first * sine], axis=-1)

def tables(positions):
    half = ROPE // 2
    freqs = 10000.0 ** (-jnp.arange(half, dtype=jnp.float32) * 2.0 / ROPE)
    angles = positions[:, None] * freqs[None, :]
    return (jnp.cos(angles), jnp.sin(angles))

def rms_scale(values, gain):
    return values * lax.rsqrt(lax.optimization_barrier(jnp.mean(values * values, axis=-1, keepdims=True)) + EPS) * gain

def matmul(left, right):
    return jnp.dot(left, right, precision=HIGH, preferred_element_type=jnp.float32)

def sequence_layer(weights, tokens):
    gain_one, gain_two, gain_query, gain_keys, latent_w, query_w, keys_w, output_w, gate_w, upper_w, down_w = weights
    cosine, sine = tables(jnp.arange(SEQ, dtype=jnp.float32))
    scale = 1.0 / math.sqrt(NOPE + ROPE)
    normed = low(rms_scale(tokens, gain_one))
    latent = low_back(matmul(normed, latent_w))
    query_lat = low(rms_scale(latent[:, :QR], gain_query))
    keys_lat = low(rms_scale(latent[:, QR:QR + KVR], gain_keys))
    shared_rot = low(rotate(latent[:, QR + KVR:], cosine, sine))
    query_raw = low_back(matmul(query_lat, query_w)).reshape(SEQ, HEADS, NOPE + ROPE)
    queries = low(jnp.concatenate([query_raw[..., :NOPE], rotate(query_raw[..., NOPE:], cosine[:, None, :], sine[:, None, :])], axis=-1))
    keys_raw = low_back(matmul(keys_lat, keys_w)).reshape(SEQ, HEADS, NOPE + VDIM)
    keys_full = jnp.concatenate([low(keys_raw[..., :NOPE]), jnp.broadcast_to(shared_rot[:, None, :], (SEQ, HEADS, ROPE))], axis=-1)
    values_all = low(keys_raw[..., NOPE:])
    scores = low_back(jnp.einsum('qhd,khd->hqk', queries, keys_full, precision=HIGH) * scale)
    causal = jnp.arange(SEQ)[:, None] >= jnp.arange(SEQ)[None, :]
    scores = jnp.where(causal[None], scores, -1e+30)
    shifted = scores - lax.optimization_barrier(jnp.max(scores, axis=-1, keepdims=True))
    expo = jnp.exp(shifted)
    probs = low(expo / lax.optimization_barrier(jnp.sum(expo, axis=-1, keepdims=True)))
    attended = low(low_back(jnp.einsum('hqk,khd->qhd', probs, values_all, precision=HIGH))).reshape(SEQ, HEADS * VDIM)
    branch = low_back(matmul(attended, output_w))
    hidden_state = tokens + RESIDUAL * branch
    mlp_in = low(rms_scale(hidden_state, gain_two))
    gate = low_back(matmul(mlp_in, gate_w))
    upper = low_back(matmul(mlp_in, upper_w))
    hidden = low(gate * jax.nn.sigmoid(gate) * upper)
    return hidden_state + RESIDUAL * low_back(matmul(hidden, down_w))

def forward(gains, latent_w, query_w, keys_w, output_w, gate_w, upper_w, down_w, inputs):
    low_gains = low(gains)
    weights = (low_gains[:D], low_gains[D:2 * D], low_gains[2 * D:2 * D + QR], low_gains[2 * D + QR:], low(latent_w), low(query_w), low(keys_w), low(output_w), low(gate_w), low(upper_w), low(down_w))

    def one_sequence(block):
        return sequence_layer(weights, block)
    outputs = lax.map(jax.checkpoint(one_sequence), inputs.reshape(N_DP, SEQ, D))
    return outputs.reshape(N_DP * SEQ, D)

def adamw(weight, grad, moment, second, rate, decay):
    moment_new = BETA_ONE * moment + (1.0 - BETA_ONE) * grad
    second_new = BETA_TWO * second + (1.0 - BETA_TWO) * grad * grad
    corr_one = 1.0 - BETA_ONE ** STEP
    corr_two = 1.0 - BETA_TWO ** STEP
    stepped = moment_new / corr_one / (jnp.sqrt(second_new / corr_two) + ADAM_EPS)
    return (weight - rate * (stepped + decay * weight), moment_new, second_new)

def rate_table():
    return (2.0, 3.0 / math.sqrt(D), 3.0 / math.sqrt(QR), 3.0 / math.sqrt(KVR), 3.0 / math.sqrt(HEADS * VDIM // 256), 3.0 / math.sqrt(D), 3.0 / math.sqrt(D), 3.0 / math.sqrt(FF // 64))

def reference(block_input, out_grad, norm_gains, latent_weight, query_weight, keys_weight, output_weight, gate_weight, up_weight, down_weight, gains_moment, gains_second, latent_moment, latent_second, query_moment, query_second, keys_moment, keys_second, output_moment, output_second, gate_moment, gate_second, up_moment, up_second, down_moment, down_second):
    block_output, pullback = jax.vjp(forward, norm_gains, latent_weight, query_weight, keys_weight, output_weight, gate_weight, up_weight, down_weight, block_input.astype(jnp.float32))
    grads = pullback(out_grad.astype(jnp.float32))
    rates = rate_table()
    next_gains, moment_gains, second_gains = adamw(norm_gains, grads[0], gains_moment, gains_second, rates[0], 0.0)
    next_latent, moment_latent, second_latent = adamw(latent_weight, grads[1], latent_moment, latent_second, rates[1], 0.1)
    next_query, moment_query, second_query = adamw(query_weight, grads[2], query_moment, query_second, rates[2], 0.1)
    next_keys, moment_keys, second_keys = adamw(keys_weight, grads[3], keys_moment, keys_second, rates[3], 0.1)
    next_output, moment_output, second_output = adamw(output_weight, grads[4], output_moment, output_second, rates[4], 0.1)
    next_gate, moment_gate, second_gate = adamw(gate_weight, grads[5], gate_moment, gate_second, rates[5], 0.1)
    next_up, moment_up, second_up = adamw(up_weight, grads[6], up_moment, up_second, rates[6], 0.1)
    next_down, moment_down, second_down = adamw(down_weight, grads[7], down_moment, down_second, rates[7], 0.1)
    input_grad = grads[8]
    return (block_output, input_grad, next_gains, moment_gains, second_gains, next_latent, moment_latent, second_latent, next_query, moment_query, second_query, next_keys, moment_keys, second_keys, next_output, moment_output, second_output, next_gate, moment_gate, second_gate, next_up, moment_up, second_up, next_down, moment_down, second_down)
```

```python
import math

import jax
import jax.numpy as jnp
from jax import lax
from jax.experimental import pallas as pl
from jax.experimental.pallas import tpu as pltpu
from jax.sharding import PartitionSpec as P

D = 2560
HEADS = 40
NOPE = 64
ROPE = 32
VDIM = 64
QR = 768
KVR = 256
FF = 6400
STEP = 10
RING = 4
SLICE = 320
LANES = 128
CELL = 256
BLOCK = 512
AXES = ("yl", "x", "c", "yh", "z")
SIZES = (2, 4, 2, 2, 4)
PLANE = ("yl", "x", "yh")


EPS = 1e-05
RESIDUAL = 1.4 / math.sqrt(62.0)
BETA_ONE = 0.9
BETA_TWO = 0.95
ADAM_EPS = 1e-08


def to_low(values):
    return values.astype(jnp.bfloat16)


def rotate(values, cosine, sine):
    half = values.shape[-1] // 2
    first = values[..., :half]
    second = values[..., half:]
    return jnp.concatenate(
        [first * cosine - second * sine, second * cosine + first * sine], axis=-1
    )


def unrotate(grads, cosine, sine):
    half = grads.shape[-1] // 2
    first = grads[..., :half]
    second = grads[..., half:]
    return jnp.concatenate(
        [first * cosine + second * sine, second * cosine - first * sine], axis=-1
    )


def tables(positions):
    half = ROPE // 2
    freqs = 10000.0 ** (-jnp.arange(half, dtype=jnp.float32) * 2.0 / ROPE)
    angles = positions[:, None] * freqs[None, :]
    return (jnp.cos(angles), jnp.sin(angles))


def rms_forward(values, gain):
    factor = lax.rsqrt(jnp.mean(values * values, axis=-1, keepdims=True) + EPS)
    return (values * factor * gain, factor)


def rms_backward(grad_out, values, factor, gain):
    scaled = grad_out * gain
    width = values.shape[-1]
    inner = jnp.sum(scaled * values, axis=-1, keepdims=True) / width
    grad_in = factor * scaled - values * factor * factor * factor * inner
    grad_gain = jnp.sum(grad_out * values * factor, axis=0)
    return (grad_in, grad_gain)


def adamw(weight, grad, moment, second, rate, decay):
    moment_new = BETA_ONE * moment + (1.0 - BETA_ONE) * grad
    second_new = BETA_TWO * second + (1.0 - BETA_TWO) * grad * grad
    corr_one = 1.0 - BETA_ONE**STEP
    corr_two = 1.0 - BETA_TWO**STEP
    stepped = moment_new / corr_one / (jnp.sqrt(second_new / corr_two) + ADAM_EPS)
    return (weight - rate * (stepped + decay * weight), moment_new, second_new)


def rate_table():
    return (
        2.0,
        3.0 / math.sqrt(D),
        3.0 / math.sqrt(QR),
        3.0 / math.sqrt(KVR),
        3.0 / math.sqrt(HEADS * VDIM // 256),
        3.0 / math.sqrt(D),
        3.0 / math.sqrt(D),
        3.0 / math.sqrt(FF // 64),
    )


def ring(step):
    return [(place, (place + step) % RING) for place in range(RING)]


def send_z(block, step):
    return lax.ppermute(block, "z", ring(step))


def send_x(block, step):
    return lax.ppermute(block, "x", ring(step))


def send_y(block, step):
    pairs = [(a % 2 * 2 + a // 2, b % 2 * 2 + b // 2) for a, b in ring(step)]
    return lax.ppermute(block, ("yl", "yh"), pairs)


def send_core(block):
    return lax.ppermute(block, "c", [(0, 1), (1, 0)])


def swap(block):
    return lax.ppermute(block, ("c", "yh"), [(0, 0), (1, 2), (2, 1), (3, 3)])


def pick(place, rel, index):
    return lax.select_n(place, *[rel[(own - index) % RING] for own in range(RING)])


def in_order(place, rel):
    return [pick(place, rel, index) for index in range(RING)]


def tie(keep, *others):
    anywhere = pl.BlockSpec(memory_space=pl.ANY)
    count = len(keep)
    return pl.pallas_call(
        lambda *refs: None,
        in_specs=[anywhere] * (count + len(others)),
        out_specs=[anywhere] * count,
        out_shape=[jax.ShapeDtypeStruct(array.shape, array.dtype) for array in keep],
        input_output_aliases={index: index for index in range(count)},
        name="tie",
    )(*keep, *others)


def gather_group(block):
    half = block.shape[0] // 2
    after, before = send_z(block, 1), send_z(block, -1)
    across = jnp.concatenate([send_z(after[:half], 1), send_z(before[half:], -1)], axis=0)
    return [(part, send_core(part)) for part in (block, after, across, before)]


def joined(pairs):
    return jnp.concatenate([part for pair in pairs for part in pair], axis=0)


def scatter_ring(sums):
    half = sums[0].shape[0] // 2
    across = to_low(sums[2])
    down = send_z(across[:half], -1).astype(jnp.float32)
    up = send_z(across[half:], 1).astype(jnp.float32)
    after = jnp.concatenate([sums[1][:half] + down, sums[1][half:]], axis=0)
    before = jnp.concatenate([sums[3][:half], sums[3][half:] + up], axis=0)
    return (
        sums[0]
        + send_z(to_low(after), -1).astype(jnp.float32)
        + send_z(to_low(before), 1).astype(jnp.float32)
    )


def scatter_group(pairs):
    return scatter_ring(
        [mine.astype(jnp.float32) + send_core(other).astype(jnp.float32) for mine, other in pairs]
    )


def scatter_halves(mine, other):
    rows = mine.shape[0] // RING
    sums = mine.astype(jnp.float32) + send_core(other).astype(jnp.float32)
    return scatter_ring([sums[rows * step : rows * (step + 1)] for step in range(RING)])


def to_abs(mine, other, place):
    mine = jnp.concatenate(in_order(place["z"], mine), axis=0)
    other = jnp.concatenate(in_order(place["z"], other), axis=0)
    first = place["c"] == 0
    return jnp.concatenate(
        [jnp.where(first, mine, other), jnp.where(first, other, mine)], axis=0
    )


def to_rel(rows, place):
    size = rows.shape[0] // (2 * RING)
    halves = []
    for core in (place["c"], 1 - place["c"]):
        spots = [(place["z"] - step) % RING for step in range(RING)]
        halves.append(
            jnp.concatenate(
                [
                    lax.dynamic_slice_in_dim(rows, (core * RING + spot) * size, size, axis=0)
                    for spot in spots
                ],
                axis=0,
            )
        )
    return halves


def empty(shape):
    return pl.pallas_call(
        lambda ref: None,
        out_specs=pl.BlockSpec(memory_space=pl.ANY),
        out_shape=jax.ShapeDtypeStruct(shape, jnp.bfloat16),
        name="empty",
    )()


def line_y(blocks):
    return [blocks[0], blocks[2], blocks[1], blocks[3]]


def spot_y(place, step):
    spot = (place["y"] + step) % RING
    return spot % 2 * 2 + spot // 2


def spot_x(place, step):
    return (place["x"] + step) % RING


def first_x(block, place):
    return jnp.stack(in_order(place["x"], [block] + [send_x(block, s) for s in (1, 2, 3)]))


def first_y(block, place):
    near = [block] + [send_y(block, s) for s in (1, 2, 3)]
    return jnp.stack(line_y(in_order(place["y"], near)))


def second(line, place, send, spot):
    half = line.shape[0] // 2
    after, before = send(line, 1), send(line, -1)
    across = jnp.concatenate([send(after[:half], 1), send(before[half:], -1)], axis=0)
    out = empty((RING,) + line.shape)
    zeros = (0,) * line.ndim
    for step, part in enumerate((line, after, across, before)):
        out = lax.dynamic_update_slice(out, part[None], (spot(place, -step),) + zeros)
    return out


def second_y(line, place):
    return second(line, place, send_y, spot_y)


def second_x(line, place):
    return second(line, place, send_x, spot_x)


def fold(blocks, place, send, spot):
    def at(step):
        return lax.dynamic_index_in_dim(blocks, spot(place, step), axis=0, keepdims=False)

    across, after, before = at(2), at(1), at(3)
    half = across.shape[0] // 2
    up = send(across[:half], 1).astype(jnp.float32)
    down = send(across[half:], -1).astype(jnp.float32)
    after = after.astype(jnp.float32)
    before = before.astype(jnp.float32)
    after = to_low(jnp.concatenate([after[:half] + up, after[half:]], axis=0))
    before = to_low(jnp.concatenate([before[:half], before[half:] + down], axis=0))
    parts = (at(0), send(after, 1), send(before, -1))
    return to_low(sum(part.astype(jnp.float32) for part in parts))


def fold_x(blocks, place):
    return fold(blocks, place, send_x, spot_x)


def fold_y(blocks, place):
    return fold(blocks, place, send_y, spot_y)


def routes(x_first):
    pairs = []
    for source in range(32):
        rest, at_yh = divmod(source, 2)
        rest, at_c = divmod(rest, 2)
        at_yl, at_x = divmod(rest, 4)
        row = at_yl * 8 + at_x * 2 + at_c
        if x_first:
            to_yl, to_yh, to_x = row // 8, row // 4 % 2, row % 4
        else:
            to_x, to_yl, to_yh = row // 4, row // 2 % 2, row % 2
        pairs.append((source, ((to_yl * 4 + to_x) * 2 + at_yh) * 2 + to_yh))
    return pairs


def trade(block, x_first):
    return lax.ppermute(block, ("yl", "x", "c", "yh"), routes(x_first))


def trade_back(block, x_first):
    back = [(target, source) for source, target in routes(x_first)]
    return lax.ppermute(block, ("yl", "x", "c", "yh"), back)


def by_four(blocks, names):
    return lax.all_to_all(blocks, names, split_axis=0, concat_axis=0, tiled=True)


def four_copies(block):
    return jnp.broadcast_to(block[None], (RING,) + block.shape)


def ff_kernel(*refs):
    parts, (grad_ref, weight_ref, rest_ref), backs = refs[:4], refs[4:7], refs[-8:-4]
    rows_ref, hidden_ref, both_ref, total = refs[-4:]
    step = pl.program_id(0)
    last = pl.num_programs(0) - 1
    size = parts[0].shape[0]

    @pl.when(step == 0)
    def _():
        for index, part in enumerate(parts):
            rows_ref[index * size : (index + 1) * size] = part[...]

    def columns(source, half):
        weight = source[...]
        both = jnp.dot(rows_ref[...], weight, preferred_element_type=jnp.float32)
        gate, upper = both[:, :half], both[:, half:]
        grad = grad_ref[:, :half]
        sigma = jax.nn.sigmoid(gate)
        hidden_ref[:, :half] = to_low(gate * sigma * upper)
        grads = jnp.concatenate(
            [
                to_low(grad * upper * sigma * (1.0 + gate * (1.0 - sigma))),
                to_low(grad * gate * sigma),
            ],
            axis=1,
        )
        both_ref[:, : 2 * half] = grads
        return lax.dot_general(
            grads, weight, (((1,), (1,)), ((), ())), preferred_element_type=jnp.float32
        )

    @pl.when(step == 0)
    def _():
        total[...] = columns(weight_ref, CELL)

    @pl.when((step > 0) & (step < last))
    def _():
        total[...] += columns(weight_ref, CELL)

    @pl.when(step == last)
    def _():
        result = total[...] + columns(rest_ref, CELL // 2)
        for index, back in enumerate(backs):
            back[...] = to_low(result[index * size : (index + 1) * size])


def feed_forward(parts, grad_hidden, weights, rest, held, spot):
    size, width = parts[0].shape
    rows, columns = 4 * size, weights.shape[1] + CELL
    steps = pl.cdiv(columns, 2 * CELL)
    count = 2 * RING * size
    whole = pl.BlockSpec((size, width), lambda j: (0, 0))
    anywhere = pl.BlockSpec(memory_space=pl.ANY)
    return pl.pallas_call(
        ff_kernel,
        grid=(steps,),
        in_specs=[whole] * 4
        + [
            pl.BlockSpec((rows, CELL), lambda j: (spot, j)),
            pl.BlockSpec((width, 2 * CELL), lambda j: (0, jnp.minimum(j, steps - 2))),
            pl.BlockSpec((width, CELL), lambda j: (0, 0)),
        ]
        + [anywhere] * len(held),
        out_specs=[whole] * 4
        + [
            pl.BlockSpec((rows, width), lambda j: (spot, 0)),
            pl.BlockSpec((rows, CELL), lambda j: (spot, j)),
            pl.BlockSpec((rows, 2 * CELL), lambda j: (spot, j)),
        ],
        out_shape=[jax.ShapeDtypeStruct((size, width), jnp.bfloat16)] * 4
        + [
            jax.ShapeDtypeStruct((count, width), jnp.bfloat16),
            jax.ShapeDtypeStruct((count, columns // 2), jnp.bfloat16),
            jax.ShapeDtypeStruct((count, columns), jnp.bfloat16),
        ],
        scratch_shapes=[pltpu.VMEM((rows, width), jnp.float32)],
        input_output_aliases={7 + index: 4 + index for index in range(len(held))},
        compiler_params=pltpu.CompilerParams(vmem_limit_bytes=48 << 20),
        cost_estimate=pl.CostEstimate(
            flops=4 * rows * width * columns,
            bytes_accessed=20 << 20,
            transcendentals=rows * columns // 2,
        ),
        name="feed_forward",
    )(*parts, grad_hidden, weights, rest, *held)


def mix(gate, upper):
    parts = []
    for begin in range(0, gate.shape[1], CELL):
        parts += [gate[:, begin : begin + CELL], upper[:, begin : begin + CELL]]
    return jnp.concatenate(parts, axis=1)


def unmix(both):
    sides = ([], [])
    count = both.shape[1] // 2
    for begin in range(0, count, CELL):
        half = min(CELL, count - begin)
        for index in (0, 1):
            spot = 2 * begin + index * half
            sides[index].append(both[:, spot : spot + half])
    return [jnp.concatenate(side, axis=1) for side in sides]


def scatter_plane(blocks):
    return add_up(exchange_plane(blocks))


def exchange_plane(blocks):
    return lax.all_to_all(blocks, PLANE, split_axis=0, concat_axis=0, tiled=True)


def add_up(terms):
    return to_low(jnp.sum(terms.astype(jnp.float32), axis=0))


def rope_slots(seq_rows):
    cosine, sine = tables(jnp.arange(seq_rows, dtype=jnp.float32))
    half = ROPE // 2
    one = jnp.ones((seq_rows, NOPE), jnp.float32)
    none = jnp.zeros((seq_rows, half), jnp.float32)
    plain = jnp.zeros((seq_rows, NOPE), jnp.float32)
    own = jnp.concatenate([one, cosine, cosine, none, none], axis=1)
    later = jnp.concatenate([plain, -sine, none, none, none], axis=1)
    earlier = jnp.concatenate([plain, none, sine, none, none], axis=1)
    return own, later, earlier


def turn(values, own, later, earlier):
    half = ROPE // 2
    return (
        values * own
        + pltpu.roll(values, LANES - half, 1) * later
        + pltpu.roll(values, half, 1) * earlier
    )


def attention_kernel(
    query_ref, keys_ref, wq_ref, wk_ref, own_ref, later_ref, earlier_ref, shared_ref,
    q_ref, k_ref, kv_ref, out_ref,
):
    seq_rows = query_ref.shape[0]
    heads = wq_ref.shape[1] // LANES
    scale = 1.0 / math.sqrt(NOPE + ROPE)
    lane = lax.broadcasted_iota(jnp.int32, (seq_rows, LANES), 1)
    rows = lax.broadcasted_iota(jnp.int32, (BLOCK, BLOCK), 0)
    cols = lax.broadcasted_iota(jnp.int32, (BLOCK, BLOCK), 1)
    query_raw = jnp.dot(query_ref[...], wq_ref[...], preferred_element_type=jnp.float32)
    keys_raw = jnp.dot(keys_ref[...], wk_ref[...], preferred_element_type=jnp.float32)
    for head in range(heads):
        slot = slice(head * LANES, (head + 1) * LANES)
        q = to_low(turn(query_raw[:, slot], own_ref[...], later_ref[...], earlier_ref[...]))
        kv = to_low(keys_raw[:, slot])
        k = jnp.where(lane < NOPE, kv, shared_ref[...])
        q_ref[:, slot] = q
        k_ref[:, slot] = k
        kv_ref[:, slot] = kv
        for begin in range(0, seq_rows, BLOCK):
            end = begin + BLOCK
            logits = (
                lax.dot_general(
                    q[begin:end], k[:end], (((1,), (1,)), ((), ())),
                    preferred_element_type=jnp.float32,
                )
                * scale
            )
            edge = jnp.where(rows >= cols, logits[:, begin:], -1e30)
            logits = jnp.concatenate([logits[:, :begin], edge], axis=1) if begin else edge
            peak = jnp.max(logits, axis=1, keepdims=True)
            expo = jnp.exp(logits - peak)
            probs = to_low(expo * (1.0 / jnp.sum(expo, axis=1, keepdims=True)))
            found = jnp.dot(probs, kv[:end], preferred_element_type=jnp.float32)
            out_ref[begin:end, head * VDIM : (head + 1) * VDIM] = to_low(found[:, NOPE:])


def attention(query_lat, keys_lat, wq, wk, factors, shared):
    seq_rows = query_lat.shape[0]
    heads = wq.shape[1] // LANES
    whole = pl.BlockSpec(memory_space=pltpu.VMEM)
    wide = jax.ShapeDtypeStruct((seq_rows, heads * LANES), jnp.bfloat16)
    pairs = heads * seq_rows * seq_rows
    return pl.pallas_call(
        attention_kernel,
        in_specs=[whole] * 8,
        out_specs=[whole] * 4,
        out_shape=[wide] * 3 + [jax.ShapeDtypeStruct((seq_rows, heads * VDIM), jnp.bfloat16)],
        compiler_params=pltpu.CompilerParams(vmem_limit_bytes=48 << 20),
        cost_estimate=pl.CostEstimate(
            flops=512 * pairs, bytes_accessed=8 << 20, transcendentals=pairs // 2
        ),
        name="attention",
    )(query_lat, keys_lat, wq, wk, *factors, shared)


def attention_back_kernel(
    q_ref, k_ref, kv_ref, grad_ref, own_ref, later_ref, earlier_ref,
    dq_ref, dkv_ref, shared_ref, key_total, value_total,
):
    seq_rows = q_ref.shape[0]
    heads = q_ref.shape[1] // LANES
    scale = 1.0 / math.sqrt(NOPE + ROPE)
    lane = lax.broadcasted_iota(jnp.int32, (seq_rows, LANES), 1)
    rows = lax.broadcasted_iota(jnp.int32, (BLOCK, BLOCK), 0)
    cols = lax.broadcasted_iota(jnp.int32, (BLOCK, BLOCK), 1)
    for head in range(heads):
        slot = slice(head * LANES, (head + 1) * LANES)
        q, k, kv = q_ref[:, slot], k_ref[:, slot], kv_ref[:, slot]
        grad = grad_ref[:, head * VDIM : (head + 1) * VDIM]
        grad = jnp.concatenate([jnp.zeros_like(grad), grad], axis=1)
        key_total[...] = jnp.zeros_like(key_total)
        value_total[...] = jnp.zeros_like(value_total)
        for begin in range(0, seq_rows, BLOCK):
            end = begin + BLOCK
            q_here, grad_here = q[begin:end], grad[begin:end]
            turned = (((1,), (1,)), ((), ()))
            logits = (
                lax.dot_general(k[:end], q_here, turned, preferred_element_type=jnp.float32)
                * scale
            )
            edge = jnp.where(cols >= rows, logits[begin:], -1e30)
            logits = jnp.concatenate([logits[:begin], edge], axis=0) if begin else edge
            peak = jnp.max(logits, axis=0, keepdims=True)
            expo = jnp.exp(logits - peak)
            probs = expo * (1.0 / jnp.sum(expo, axis=0, keepdims=True))
            grad_probs = lax.dot_general(
                kv[:end], grad_here, turned, preferred_element_type=jnp.float32
            )
            inner = jnp.sum(probs * grad_probs, axis=0, keepdims=True)
            grad_logits = to_low(probs * (grad_probs - inner))
            key_total[:end] += jnp.dot(grad_logits, q_here, preferred_element_type=jnp.float32)
            value_total[:end] += jnp.dot(
                to_low(probs), grad_here, preferred_element_type=jnp.float32
            )
            found = (
                lax.dot_general(
                    grad_logits, k[:end], (((0,), (0,)), ((), ())),
                    preferred_element_type=jnp.float32,
                )
                * scale
            )
            dq_ref[begin:end, slot] = to_low(
                turn(found, own_ref[begin:end], -later_ref[begin:end], -earlier_ref[begin:end])
            )
        keys = key_total[...] * scale
        dkv_ref[:, slot] = to_low(jnp.where(lane < NOPE, keys, value_total[...]))
        if head:
            shared_ref[...] += keys
        else:
            shared_ref[...] = keys


def attention_back(q, k, kv, grad, factors):
    seq_rows, width = q.shape
    whole = pl.BlockSpec(memory_space=pltpu.VMEM)
    wide = jax.ShapeDtypeStruct((seq_rows, width), jnp.bfloat16)
    pairs = width // LANES * seq_rows * seq_rows
    total = pltpu.VMEM((seq_rows, LANES), jnp.float32)
    return pl.pallas_call(
        attention_back_kernel,
        in_specs=[whole] * 7,
        out_specs=[whole] * 3,
        out_shape=[wide, wide, jax.ShapeDtypeStruct((seq_rows, LANES), jnp.float32)],
        scratch_shapes=[total, total],
        compiler_params=pltpu.CompilerParams(vmem_limit_bytes=48 << 20),
        cost_estimate=pl.CostEstimate(
            flops=1280 * pairs, bytes_accessed=10 << 20, transcendentals=pairs // 2
        ),
        name="attention_back",
    )(q, k, kv, grad, *factors)


def to_slots(weight):
    rows = weight.shape[0]
    return jnp.pad(
        weight.reshape(rows, -1, NOPE + ROPE), ((0, 0), (0, 0), (0, LANES - NOPE - ROPE))
    ).reshape(rows, -1)


def from_slots(weight):
    rows = weight.shape[0]
    return weight.reshape(rows, -1, LANES)[:, :, : NOPE + ROPE].reshape(rows, -1)


def pack_rows(block, wide):
    rows, columns = block.shape
    parts = block.reshape(rows // 16, 16, columns)
    parts = jnp.pad(parts, ((0, 0), (0, 0), (0, wide - columns)))
    return parts.transpose(1, 0, 2).reshape(16, -1)


def unpack_rows(packed, wide, columns):
    count = packed.shape[2] // wide
    parts = packed.reshape(packed.shape[0], 16, count, wide)[..., :columns]
    return parts.transpose(0, 2, 1, 3).reshape(packed.shape[0], -1, columns)


def shards(
    block_input,
    out_grad,
    norm_gains,
    latent_weight,
    query_weight,
    keys_weight,
    output_weight,
    gate_weight,
    up_weight,
    down_weight,
    gains_moment,
    gains_second,
    latent_moment,
    latent_second,
    query_moment,
    query_second,
    keys_moment,
    keys_second,
    output_moment,
    output_second,
    gate_moment,
    gate_second,
    up_moment,
    up_second,
    down_moment,
    down_second,
):
    place = {name: lax.axis_index(name) for name in AXES}
    place["y"] = place["yh"] * 2 + place["yl"]
    group_index = place["c"] * RING + place["z"]
    tok_rows = block_input.shape[0]
    seq_rows = tok_rows * 2 * RING
    heads_here = output_weight.shape[0] // VDIM
    width = QR + KVR + ROPE
    gain_width = norm_gains.shape[0]

    latent_rows = latent_weight.shape[0]
    latent_pad = 24 - latent_rows
    gain_row = jnp.pad(to_low(norm_gains)[None], ((0, latent_pad - 1), (0, width - gain_width)))
    latent_block = jnp.concatenate([to_low(latent_weight), gain_row], axis=0)
    latent_mine = lax.all_to_all(
        jnp.broadcast_to(latent_block[None], (64,) + latent_block.shape),
        PLANE + ("z",),
        split_axis=0,
        concat_axis=0,
        tiled=True,
    )
    wide = heads_here * LANES
    key_cols = keys_weight.shape[1]
    small = swap(
        jnp.concatenate(
            [
                pack_rows(to_slots(to_low(query_weight)), wide),
                to_low(keys_weight),
                pack_rows(to_low(output_weight).T, 384),
            ],
            axis=1,
        )
    )
    tokens = swap(block_input).astype(jnp.float32)
    hidden_here = gate_weight.shape[1]
    fill = -hidden_here % LANES
    both = mix(
        *[jnp.pad(to_low(weight), ((0, 0), (0, fill))) for weight in (gate_weight, up_weight)]
    )
    cut = both.shape[1] - CELL
    weights_one = both[:, :cut]
    weights_two = jnp.pad(to_low(down_weight).T, ((0, 0), (0, fill)))
    weights_two = jnp.concatenate([both[:, cut:], weights_two], axis=1)
    weights_one = trade(weights_one, True)
    weights_two = trade(weights_two, False)
    cotangent = swap(out_grad)
    own_pos = (group_index * tok_rows + jnp.arange(tok_rows)).astype(jnp.float32)
    own_cos, own_sin = tables(own_pos)
    factor_one = lax.rsqrt(jnp.mean(tokens * tokens, axis=-1, keepdims=True) + EPS)
    spaced = tokens * factor_one
    spaced = jnp.pad(
        spaced.reshape(tok_rows, 8, 2, 8, latent_rows),
        ((0, 0), (0, 0), (0, 0), (0, 0), (0, latent_pad)),
    )
    core_first = place["c"] == 0
    spaced_mine = jnp.where(core_first, spaced[:, :, 0], spaced[:, :, 1]).reshape(tok_rows, -1)
    spaced_other = jnp.where(core_first, spaced[:, :, 1], spaced[:, :, 0]).reshape(tok_rows, -1)
    small = jnp.broadcast_to(small[None], (16,) + small.shape)
    latent_mine, spaced_mine, spaced_other, small = tie(
        [latent_mine, spaced_mine, spaced_other, small], weights_one, weights_two, cotangent
    )
    latent_other = send_core(latent_mine)
    small = exchange_plane(small)

    def in_cores(mine, other, extra):
        first = jnp.where(core_first, mine, other).reshape((8, 8) + extra)
        second = jnp.where(core_first, other, mine).reshape((8, 8) + extra)
        return jnp.stack([first, second], axis=1)

    gains_all = in_cores(
        latent_mine[:, latent_rows, :gain_width],
        latent_other[:, latent_rows, :gain_width],
        (gain_width,),
    )
    gains_all = gains_all.astype(jnp.float32).reshape(-1)
    gain_one = gains_all[:D]
    gain_two = gains_all[D : 2 * D]
    gain_query = gains_all[2 * D : 2 * D + QR]
    gain_keys = gains_all[2 * D + QR :]
    latent_full = in_cores(
        latent_mine[:, :latent_rows], latent_other[:, :latent_rows], (latent_rows, width)
    ).reshape(-1, width)

    normed = to_low(tokens * factor_one * gain_one)
    spaced_gain = jnp.pad(
        gain_one.reshape(8, 2, 8, latent_rows), ((0, 0), (0, 0), (0, 0), (0, latent_pad))
    )
    gain_mine = jnp.where(core_first, spaced_gain[:, 0], spaced_gain[:, 1]).reshape(-1)
    gain_other = jnp.where(core_first, spaced_gain[:, 1], spaced_gain[:, 0]).reshape(-1)
    latent = jnp.dot(
        to_low(spaced_mine * gain_mine),
        latent_mine.reshape(-1, width),
        preferred_element_type=jnp.float32,
    ) + jnp.dot(
        to_low(spaced_other * gain_other),
        latent_other.reshape(-1, width),
        preferred_element_type=jnp.float32,
    )
    query_part = latent[:, :QR]
    keys_part = latent[:, QR : QR + KVR]
    query_pre, factor_query = rms_forward(query_part, gain_query)
    keys_pre, factor_keys = rms_forward(keys_part, gain_keys)
    packed = jnp.concatenate(
        [
            to_low(query_pre),
            to_low(keys_pre),
            to_low(rotate(latent[:, QR + KVR :], own_cos, own_sin)),
        ],
        axis=1,
    )
    packed_pairs = gather_group(packed)
    cotangent = cotangent.astype(jnp.float32)
    gathered = to_abs([p[0] for p in packed_pairs], [p[1] for p in packed_pairs], place)
    cot_block = to_low(RESIDUAL * cotangent)
    gathered, cot_block, small, weights_one, weights_two = tie(
        [gathered, cot_block, small, weights_one, weights_two]
    )
    line_one = by_four(four_copies(weights_one), "x")
    line_two = first_y(weights_two, place)
    cot_all = joined(gather_group(cot_block))
    query_full = unpack_rows(small[:, :, : 3 * wide], wide, wide).reshape(-1, wide)
    keys_matrix = small[:, :, 3 * wide : 3 * wide + key_cols].reshape(-1, key_cols)
    output_turned = unpack_rows(small[:, :, 3 * wide + key_cols :], 384, SLICE).reshape(-1, SLICE)
    query_lat = gathered[:, :QR]
    keys_lat = gathered[:, QR : QR + KVR]
    shared_rot = gathered[:, QR + KVR :]
    factors = rope_slots(seq_rows)
    shared_slot = jnp.pad(shared_rot, ((0, 0), (NOPE, LANES - NOPE - ROPE)))
    queries, keys_all, keys_values, attended = attention(
        query_lat, keys_lat, query_full, keys_matrix, factors, shared_slot
    )
    attended, line_one, line_two, cot_all = tie([attended, line_one, line_two, cot_all])
    weights_one = by_four(four_copies(line_one), ("yl", "yh")).reshape(D, -1)
    weights_two = second_x(line_two, place).reshape(D, -1)
    down_turned = weights_two[:, CELL:]
    attended_mine, attended_other = to_rel(attended, place)

    def to_model(rows):
        return to_low(
            jnp.einsum("sa,da->sd", rows, output_turned, preferred_element_type=jnp.float32)
        )

    branch = scatter_halves(to_model(attended_mine), to_model(attended_other))
    hidden_state = tokens + RESIDUAL * branch
    mlp_pre, factor_two = rms_forward(hidden_state, gain_two)

    mlp_pairs = gather_group(to_low(mlp_pre))
    grad_hidden = jnp.dot(cot_all, down_turned, preferred_element_type=jnp.float32)
    grad_hidden, latent_full = tie([grad_hidden, latent_full])
    held, back_pairs = (), []
    for spot in (0, 1):
        near, far = mlp_pairs[2 * spot : 2 * spot + 2]
        *backs, rows, hidden, both = feed_forward(
            near + far, grad_hidden, weights_one, weights_two, held, spot
        )
        held = (rows, hidden, both)
        back_pairs += [backs[:2], backs[2:]]
    mlp_all, hidden_all, grad_both = held
    grad_mlp_in = scatter_group(back_pairs)
    grad_one = to_low(
        jnp.einsum("sd,sf->df", mlp_all, grad_both[:, :cut], preferred_element_type=jnp.float32)
    )
    grad_two = jnp.concatenate(
        [
            to_low(jnp.einsum("sd,sf->df", rows, part, preferred_element_type=jnp.float32))
            for rows, part in ((mlp_all, grad_both[:, cut:]), (cot_all, hidden_all))
        ],
        axis=1,
    )
    terms_one = by_four(grad_one.reshape(RING, -1, cut), ("yl", "yh"))
    grad_mlp_in, grad_two = tie([grad_mlp_in, grad_two], grad_one)
    fold_two = fold_x(grad_two.reshape(RING, -1, grad_two.shape[1]), place)

    grad_norm_two, grad_gain_two = rms_backward(grad_mlp_in, hidden_state, factor_two, gain_two)
    grad_state = cotangent + grad_norm_two
    branch_all = joined(gather_group(to_low(RESIDUAL * grad_state)))
    mlp_terms = [
        to_low(
            jnp.einsum(
                "sf,df->sd",
                hidden_all.reshape(RING, 2, tok_rows, -1)[:, index].reshape(RING * tok_rows, -1),
                down_turned,
                preferred_element_type=jnp.float32,
            )
        )
        for index in (0, 1)
    ]
    branch_all, *mlp_terms = tie([branch_all] + mlp_terms)
    attended_pairs = jnp.stack(
        [attended_mine.reshape(RING, tok_rows, -1), attended_other.reshape(RING, tok_rows, -1)],
        axis=1,
    ).reshape(seq_rows, -1)
    grad_output = to_low(
        jnp.einsum("sd,sa->da", branch_all, attended_pairs, preferred_element_type=jnp.float32)
    )
    grad_parts = to_low(
        jnp.dot(branch_all, output_turned, preferred_element_type=jnp.float32)
    ).reshape(RING, 2, tok_rows, -1)
    grad_attended = to_abs(
        [grad_parts[step, 0] for step in range(RING)],
        [grad_parts[step, 1] for step in range(RING)],
        place,
    )
    block_output = hidden_state + RESIDUAL * scatter_halves(*mlp_terms)
    grad_attended, normed = tie([grad_attended, normed])
    normed_cols = normed.reshape(tok_rows, 2 * RING, SLICE).transpose(1, 0, 2)
    normed_parts = []
    for step in range(RING):
        spot = (place["z"] + step) % RING
        pair = jnp.stack(
            [
                lax.dynamic_index_in_dim(normed_cols, core * RING + spot, axis=0, keepdims=False)
                for core in (place["c"], 1 - place["c"])
            ]
        )
        normed_parts.append(send_z(pair, step) if step else pair)
    normed_parts = jnp.stack(normed_parts)
    normed_all = jnp.stack([normed_parts[:, 0], send_core(normed_parts[:, 1])], axis=1)
    normed_all = normed_all.reshape(seq_rows, SLICE)
    grad_query_raw, grad_keys_raw, grad_shared = attention_back(
        queries, keys_all, keys_values, grad_attended, factors
    )
    grad_shared = grad_shared[:, NOPE : NOPE + ROPE]
    grad_query_w = to_low(
        jnp.einsum("sr,sc->rc", query_lat, grad_query_raw, preferred_element_type=jnp.float32)
    )
    grad_keys_w = to_low(
        jnp.einsum("sr,sc->rc", keys_lat, grad_keys_raw, preferred_element_type=jnp.float32)
    )
    small_grads = jnp.concatenate(
        [
            jax.vmap(lambda block: pack_rows(block, wide))(grad_query_w.reshape(16, -1, wide)),
            grad_keys_w.reshape(16, 16, key_cols),
            jax.vmap(lambda block: pack_rows(block, 384))(grad_output.reshape(16, -1, SLICE)),
        ],
        axis=2,
    )
    latent_terms = to_low(
        jnp.concatenate(
            [
                jnp.einsum(
                    "sc,rc->sr", grad_query_raw, query_full, preferred_element_type=jnp.float32
                ),
                jnp.einsum(
                    "sc,rc->sr", grad_keys_raw, keys_matrix, preferred_element_type=jnp.float32
                ),
                grad_shared,
            ],
            axis=1,
        )
    )
    latent_terms, block_output, small_grads, terms_one, fold_two = tie(
        [latent_terms, block_output, small_grads, terms_one, fold_two]
    )
    block_output = swap(block_output)
    terms_one = by_four(add_up(terms_one).reshape(RING, -1, cut), "x")
    sum_two = trade_back(fold_y(fold_two.reshape(RING, -1, fold_two.shape[1]), place), False)
    sum_down = sum_two[:, CELL : CELL + hidden_here].astype(jnp.float32).T
    grad_latent_in = scatter_halves(*to_rel(latent_terms, place))
    grad_latent_in, small_grads, terms_one = tie([grad_latent_in, small_grads, terms_one])
    sum_one = trade_back(add_up(terms_one), True)
    sum_gate, sum_up = (
        part[:, :hidden_here].astype(jnp.float32)
        for part in unmix(jnp.concatenate([sum_one, sum_two[:, :CELL]], axis=1))
    )
    small_terms = exchange_plane(small_grads)
    grad_query_pre, grad_gain_query = rms_backward(
        grad_latent_in[:, :QR], query_part, factor_query, gain_query
    )
    grad_keys_pre, grad_gain_keys = rms_backward(
        grad_latent_in[:, QR : QR + KVR], keys_part, factor_keys, gain_keys
    )
    grad_rope = unrotate(grad_latent_in[:, QR + KVR :], own_cos, own_sin)
    grad_latent = to_low(jnp.concatenate([grad_query_pre, grad_keys_pre, grad_rope], axis=1))
    grad_normed = jnp.einsum(
        "sc,dc->sd", grad_latent, latent_full, preferred_element_type=jnp.float32
    )
    grad_norm_one, grad_gain_one = rms_backward(grad_normed, tokens, factor_one, gain_one)
    input_grad = swap(grad_state + grad_norm_one)

    latent_grads = joined(gather_group(grad_latent))
    grad_latent_w = jnp.einsum(
        "sd,sc->dc",
        normed_all,
        latent_grads,
        preferred_element_type=jnp.float32,
    )
    grad_gains = jnp.concatenate(
        [grad_gain_one, grad_gain_two, grad_gain_query, grad_gain_keys]
    ).reshape(2, RING, -1)
    gains_line = lax.dynamic_index_in_dim(grad_gains, place["c"], axis=0, keepdims=False)
    gains_line = gains_line + send_core(
        lax.dynamic_index_in_dim(grad_gains, 1 - place["c"], axis=0, keepdims=False)
    )


    def gains_at(step):
        spot = (place["z"] + step) % RING
        return lax.dynamic_index_in_dim(gains_line, spot, axis=0, keepdims=True)

    gains_sum = gains_at(0)
    for step in (1, 2, 3):
        gains_sum = gains_sum + send_z(gains_at(step), step)
    gains_rows = jnp.pad(gains_sum.reshape(16, 1, gain_width), ((0, 0), (0, 0), (0, width - gain_width)))
    last = to_low(jnp.concatenate([grad_latent_w.reshape(16, -1, width), gains_rows], axis=1))
    last, small_terms = tie([last, small_terms])
    sum_small = swap(add_up(small_terms)).astype(jnp.float32)
    sum_query = from_slots(unpack_rows(sum_small[None, :, : 3 * wide], wide, wide)[0])
    sum_keys = sum_small[:, 3 * wide : 3 * wide + key_cols]
    sum_output = unpack_rows(sum_small[None, :, 3 * wide + key_cols :], 384, SLICE)[0].T
    last = scatter_plane(last)
    route = []
    for source in range(128):
        rest, at_z = divmod(source, 4)
        rest, at_yh = divmod(rest, 2)
        rest, at_c = divmod(rest, 2)
        at_yl, at_x = divmod(rest, 4)
        route.append((source, 16 * (at_c * 4 + at_z) + (at_yl * 4 + at_x) * 2 + at_yh))
    last = lax.ppermute(last, AXES, route).astype(jnp.float32)
    sum_latent = last[:-1]
    sum_gains = last[-1, :gain_width]

    rates = rate_table()
    next_gains, moment_gains, second_gains = adamw(
        norm_gains, sum_gains, gains_moment, gains_second, rates[0], 0.0
    )
    next_latent, moment_latent, second_latent = adamw(
        latent_weight, sum_latent, latent_moment, latent_second, rates[1], 0.1
    )
    next_query, moment_query, second_query = adamw(
        query_weight, sum_query, query_moment, query_second, rates[2], 0.1
    )
    next_keys, moment_keys, second_keys = adamw(
        keys_weight, sum_keys, keys_moment, keys_second, rates[3], 0.1
    )
    next_output, moment_output, second_output = adamw(
        output_weight, sum_output, output_moment, output_second, rates[4], 0.1
    )
    next_gate, moment_gate, second_gate = adamw(
        gate_weight, sum_gate, gate_moment, gate_second, rates[5], 0.1
    )
    next_up, moment_up, second_up = adamw(
        up_weight, sum_up, up_moment, up_second, rates[6], 0.1
    )
    next_down, moment_down, second_down = adamw(
        down_weight, sum_down, down_moment, down_second, rates[7], 0.1
    )
    return (
        block_output,
        input_grad,
        next_gains,
        moment_gains,
        second_gains,
        next_latent,
        moment_latent,
        second_latent,
        next_query,
        moment_query,
        second_query,
        next_keys,
        moment_keys,
        second_keys,
        next_output,
        moment_output,
        second_output,
        next_gate,
        moment_gate,
        second_gate,
        next_up,
        moment_up,
        second_up,
        next_down,
        moment_down,
        second_down,
    )


def solution(mesh):
    devices = jax.sharding.Mesh(mesh.devices.reshape(SIZES), AXES)
    rows, split = ("yl", "x", "c"), ("yh", "z")
    whole = rows + split
    tokens, flat = P(whole, None), P(whole)
    by_rows, by_cols = P(rows, split), P(split, rows)
    weights = (flat, tokens, by_rows, by_rows, by_cols, by_rows, by_rows, by_cols)
    return jax.shard_map(
        shards,
        mesh=devices,
        in_specs=(tokens, tokens) + weights + tuple(s for s in weights for _ in range(2)),
        out_specs=(tokens, tokens) + tuple(s for s in weights for _ in range(3)),
        check_vma=False,
    )
```

```python
import math

import jax
import jax.numpy as jnp
from jax import lax
from jax.experimental import pallas as pl
from jax.experimental.pallas import tpu as pltpu
from jax.sharding import PartitionSpec as P

D = 2560
HEADS = 40
NOPE = 64
ROPE = 32
VDIM = 64
QR = 768
KVR = 256
FF = 6400
STEP = 10
RING = 4
SLICE = 320
LANES = 128
CELL = 256
BLOCK = 512
AXES = ("yl", "x", "c", "yh", "z")
SIZES = (2, 4, 2, 2, 4)
PLANE = ("yl", "x", "yh")


EPS = 1e-05
RESIDUAL = 1.4 / math.sqrt(62.0)
BETA_ONE = 0.9
BETA_TWO = 0.95
ADAM_EPS = 1e-08


def to_low(values):
    return values.astype(jnp.bfloat16)


def rotate(values, cosine, sine):
    half = values.shape[-1] // 2
    first = values[..., :half]
    second = values[..., half:]
    return jnp.concatenate(
        [first * cosine - second * sine, second * cosine + first * sine], axis=-1
    )


def unrotate(grads, cosine, sine):
    half = grads.shape[-1] // 2
    first = grads[..., :half]
    second = grads[..., half:]
    return jnp.concatenate(
        [first * cosine + second * sine, second * cosine - first * sine], axis=-1
    )


def tables(positions):
    half = ROPE // 2
    freqs = 10000.0 ** (-jnp.arange(half, dtype=jnp.float32) * 2.0 / ROPE)
    angles = positions[:, None] * freqs[None, :]
    return (jnp.cos(angles), jnp.sin(angles))


def rms_forward(values, gain):
    factor = lax.rsqrt(jnp.mean(values * values, axis=-1, keepdims=True) + EPS)
    return (values * factor * gain, factor)


def rms_backward(grad_out, values, factor, gain):
    scaled = grad_out * gain
    width = values.shape[-1]
    inner = jnp.sum(scaled * values, axis=-1, keepdims=True) / width
    grad_in = factor * scaled - values * factor * factor * factor * inner
    grad_gain = jnp.sum(grad_out * values * factor, axis=0)
    return (grad_in, grad_gain)


def adamw(weight, grad, moment, second, rate, decay):
    moment_new = BETA_ONE * moment + (1.0 - BETA_ONE) * grad
    second_new = BETA_TWO * second + (1.0 - BETA_TWO) * grad * grad
    corr_one = 1.0 - BETA_ONE**STEP
    corr_two = 1.0 - BETA_TWO**STEP
    stepped = moment_new / corr_one / (jnp.sqrt(second_new / corr_two) + ADAM_EPS)
    return (weight - rate * (stepped + decay * weight), moment_new, second_new)


def rate_table():
    return (
        2.0,
        3.0 / math.sqrt(D),
        3.0 / math.sqrt(QR),
        3.0 / math.sqrt(KVR),
        3.0 / math.sqrt(HEADS * VDIM // 256),
        3.0 / math.sqrt(D),
        3.0 / math.sqrt(D),
        3.0 / math.sqrt(FF // 64),
    )


def ring(step):
    return [(place, (place + step) % RING) for place in range(RING)]


def send_z(block, step):
    return lax.ppermute(block, "z", ring(step))


def send_x(block, step):
    return lax.ppermute(block, "x", ring(step))


def send_y(block, step):
    pairs = [(a % 2 * 2 + a // 2, b % 2 * 2 + b // 2) for a, b in ring(step)]
    return lax.ppermute(block, ("yl", "yh"), pairs)


def send_core(block):
    return lax.ppermute(block, "c", [(0, 1), (1, 0)])


def swap(block):
    return lax.ppermute(block, ("c", "yh"), [(0, 0), (1, 2), (2, 1), (3, 3)])


def pick(place, rel, index):
    return lax.select_n(place, *[rel[(own - index) % RING] for own in range(RING)])


def in_order(place, rel):
    return [pick(place, rel, index) for index in range(RING)]


def tie(keep, *others):
    anywhere = pl.BlockSpec(memory_space=pl.ANY)
    count = len(keep)
    return pl.pallas_call(
        lambda *refs: None,
        in_specs=[anywhere] * (count + len(others)),
        out_specs=[anywhere] * count,
        out_shape=[jax.ShapeDtypeStruct(array.shape, array.dtype) for array in keep],
        input_output_aliases={index: index for index in range(count)},
        name="tie",
    )(*keep, *others)


def gather_group(block):
    return gather_rest(block, send_z(block, 1), send_z(block, -1))


def gather_rest(block, after, before):
    half = block.shape[0] // 2
    across = jnp.concatenate([send_z(after[:half], 1), send_z(before[half:], -1)], axis=0)
    return [(part, send_core(part)) for part in (block, after, across, before)]


def joined(pairs):
    return jnp.concatenate([part for pair in pairs for part in pair], axis=0)


def ring_across(sums):
    half = sums[0].shape[0] // 2
    across = to_low(sums[2])
    return send_z(across[:half], -1), send_z(across[half:], 1)


def ring_near(sums, down, up):
    half = sums[0].shape[0] // 2
    after = jnp.concatenate([sums[1][:half] + down.astype(jnp.float32), sums[1][half:]], axis=0)
    before = jnp.concatenate([sums[3][:half], sums[3][half:] + up.astype(jnp.float32)], axis=0)
    return send_z(to_low(after), -1), send_z(to_low(before), 1)


def ring_finish(sums, down, up):
    after, before = ring_near(sums, down, up)
    return sums[0] + after.astype(jnp.float32) + before.astype(jnp.float32)


def halves_sums(mine, other):
    rows = mine.shape[0] // RING
    sums = mine.astype(jnp.float32) + send_core(other).astype(jnp.float32)
    return [sums[rows * step : rows * (step + 1)] for step in range(RING)]


def scatter_halves(mine, other):
    sums = halves_sums(mine, other)
    return ring_finish(sums, *ring_across(sums))


def scatter_group(pairs):
    sums = [
        mine.astype(jnp.float32) + send_core(other).astype(jnp.float32) for mine, other in pairs
    ]
    return ring_finish(sums, *ring_across(sums))


def to_abs(mine, other, place):
    mine = jnp.concatenate(in_order(place["z"], mine), axis=0)
    other = jnp.concatenate(in_order(place["z"], other), axis=0)
    first = place["c"] == 0
    return jnp.concatenate(
        [jnp.where(first, mine, other), jnp.where(first, other, mine)], axis=0
    )


def to_rel(rows, place):
    size = rows.shape[0] // (2 * RING)
    halves = []
    for core in (place["c"], 1 - place["c"]):
        spots = [(place["z"] - step) % RING for step in range(RING)]
        halves.append(
            jnp.concatenate(
                [
                    lax.dynamic_slice_in_dim(rows, (core * RING + spot) * size, size, axis=0)
                    for spot in spots
                ],
                axis=0,
            )
        )
    return halves


def empty(shape):
    return pl.pallas_call(
        lambda ref: None,
        out_specs=pl.BlockSpec(memory_space=pl.ANY),
        out_shape=jax.ShapeDtypeStruct(shape, jnp.bfloat16),
        name="empty",
    )()


def line_y(blocks):
    return [blocks[0], blocks[2], blocks[1], blocks[3]]


def spot_y(place, step):
    spot = (place["y"] + step) % RING
    return spot % 2 * 2 + spot // 2


def spot_x(place, step):
    return (place["x"] + step) % RING


def first_x(block, place):
    return jnp.stack(in_order(place["x"], [block] + [send_x(block, s) for s in (1, 2, 3)]))


def first_y(block, place):
    near = [block] + [send_y(block, s) for s in (1, 2, 3)]
    return jnp.stack(line_y(in_order(place["y"], near)))


def second(line, place, send, spot):
    half = line.shape[0] // 2
    after, before = send(line, 1), send(line, -1)
    across = jnp.concatenate([send(after[:half], 1), send(before[half:], -1)], axis=0)
    out = empty((RING,) + line.shape)
    zeros = (0,) * line.ndim
    for step, part in enumerate((line, after, across, before)):
        out = lax.dynamic_update_slice(out, part[None], (spot(place, -step),) + zeros)
    return out


def second_y(line, place):
    return second(line, place, send_y, spot_y)


def second_x(line, place):
    return second(line, place, send_x, spot_x)


def fold_across(blocks, place, send, spot):
    across = lax.dynamic_index_in_dim(blocks, spot(place, 2), axis=0, keepdims=False)
    half = across.shape[0] // 2
    return send(across[:half], 1), send(across[half:], -1)


def fold_near(blocks, up, down, place, send, spot):
    def at(step):
        return lax.dynamic_index_in_dim(blocks, spot(place, step), axis=0, keepdims=False)

    half = up.shape[0]
    after = at(1).astype(jnp.float32)
    before = at(3).astype(jnp.float32)
    after = to_low(jnp.concatenate([after[:half] + up.astype(jnp.float32), after[half:]], axis=0))
    before = to_low(
        jnp.concatenate([before[:half], before[half:] + down.astype(jnp.float32)], axis=0)
    )
    return at(0), send(after, 1), send(before, -1)


def fold(blocks, place, send, spot):
    up, down = fold_across(blocks, place, send, spot)
    return fold_sum(fold_near(blocks, up, down, place, send, spot))


def fold_sum(parts):
    return to_low(sum(part.astype(jnp.float32) for part in parts))


def fold_x(blocks, place):
    return fold(blocks, place, send_x, spot_x)


def fold_y(blocks, place):
    return fold(blocks, place, send_y, spot_y)


def routes(x_first):
    pairs = []
    for source in range(32):
        rest, at_yh = divmod(source, 2)
        rest, at_c = divmod(rest, 2)
        at_yl, at_x = divmod(rest, 4)
        row = at_yl * 8 + at_x * 2 + at_c
        if x_first:
            to_yl, to_yh, to_x = row // 8, row // 4 % 2, row % 4
        else:
            to_x, to_yl, to_yh = row // 4, row // 2 % 2, row % 2
        pairs.append((source, ((to_yl * 4 + to_x) * 2 + at_yh) * 2 + to_yh))
    return pairs


def trade(block, x_first):
    return lax.ppermute(block, ("yl", "x", "c", "yh"), routes(x_first))


def trade_back(block, x_first):
    back = [(target, source) for source, target in routes(x_first)]
    return lax.ppermute(block, ("yl", "x", "c", "yh"), back)


def by_four(blocks, names):
    return lax.all_to_all(blocks, names, split_axis=0, concat_axis=0, tiled=True)


def four_copies(block):
    return jnp.broadcast_to(block[None], (RING,) + block.shape)


def ff_kernel(*refs):
    parts, (grad_ref, weight_ref, rest_ref), backs = refs[:4], refs[4:7], refs[-8:-4]
    rows_ref, hidden_ref, both_ref, total = refs[-4:]
    step = pl.program_id(0)
    last = pl.num_programs(0) - 1
    size = parts[0].shape[0]

    @pl.when(step == 0)
    def _():
        for index, part in enumerate(parts):
            rows_ref[index * size : (index + 1) * size] = part[...]

    def columns(source, half):
        weight = source[...]
        both = jnp.dot(rows_ref[...], weight, preferred_element_type=jnp.float32)
        gate, upper = both[:, :half], both[:, half:]
        grad = grad_ref[:, :half]
        sigma = jax.nn.sigmoid(gate)
        hidden_ref[:, :half] = to_low(gate * sigma * upper)
        grads = jnp.concatenate(
            [
                to_low(grad * upper * sigma * (1.0 + gate * (1.0 - sigma))),
                to_low(grad * gate * sigma),
            ],
            axis=1,
        )
        both_ref[:, : 2 * half] = grads
        return lax.dot_general(
            grads, weight, (((1,), (1,)), ((), ())), preferred_element_type=jnp.float32
        )

    @pl.when(step == 0)
    def _():
        total[...] = columns(weight_ref, CELL)

    @pl.when((step > 0) & (step < last))
    def _():
        total[...] += columns(weight_ref, CELL)

    @pl.when(step == last)
    def _():
        result = total[...] + columns(rest_ref, CELL // 2)
        for index, back in enumerate(backs):
            back[...] = to_low(result[index * size : (index + 1) * size])


def feed_forward(parts, grad_hidden, weights, rest, held, spot):
    size, width = parts[0].shape
    rows, columns = 4 * size, weights.shape[1] + CELL
    steps = pl.cdiv(columns, 2 * CELL)
    count = 2 * RING * size
    whole = pl.BlockSpec((size, width), lambda j: (0, 0))
    anywhere = pl.BlockSpec(memory_space=pl.ANY)
    return pl.pallas_call(
        ff_kernel,
        grid=(steps,),
        in_specs=[whole] * 4
        + [
            pl.BlockSpec((rows, CELL), lambda j: (spot, j)),
            pl.BlockSpec((width, 2 * CELL), lambda j: (0, jnp.minimum(j, steps - 2))),
            pl.BlockSpec((width, CELL), lambda j: (0, 0)),
        ]
        + [anywhere] * len(held),
        out_specs=[whole] * 4
        + [
            pl.BlockSpec((rows, width), lambda j: (spot, 0)),
            pl.BlockSpec((rows, CELL), lambda j: (spot, j)),
            pl.BlockSpec((rows, 2 * CELL), lambda j: (spot, j)),
        ],
        out_shape=[jax.ShapeDtypeStruct((size, width), jnp.bfloat16)] * 4
        + [
            jax.ShapeDtypeStruct((count, width), jnp.bfloat16),
            jax.ShapeDtypeStruct((count, columns // 2), jnp.bfloat16),
            jax.ShapeDtypeStruct((count, columns), jnp.bfloat16),
        ],
        scratch_shapes=[pltpu.VMEM((rows, width), jnp.float32)],
        input_output_aliases={7 + index: 4 + index for index in range(len(held))},
        compiler_params=pltpu.CompilerParams(vmem_limit_bytes=48 << 20),
        cost_estimate=pl.CostEstimate(
            flops=4 * rows * width * columns,
            bytes_accessed=20 << 20,
            transcendentals=rows * columns // 2,
        ),
        name="feed_forward",
    )(*parts, grad_hidden, weights, rest, *held)


def mix(gate, upper):
    parts = []
    for begin in range(0, gate.shape[1], CELL):
        parts += [gate[:, begin : begin + CELL], upper[:, begin : begin + CELL]]
    return jnp.concatenate(parts, axis=1)


def unmix(both):
    sides = ([], [])
    count = both.shape[1] // 2
    for begin in range(0, count, CELL):
        half = min(CELL, count - begin)
        for index in (0, 1):
            spot = 2 * begin + index * half
            sides[index].append(both[:, spot : spot + half])
    return [jnp.concatenate(side, axis=1) for side in sides]


def scatter_plane(blocks):
    return add_up(exchange_plane(blocks))


def exchange_plane(blocks):
    return lax.all_to_all(blocks, PLANE, split_axis=0, concat_axis=0, tiled=True)


def add_up(terms):
    return to_low(jnp.sum(terms.astype(jnp.float32), axis=0))


def rope_slots(seq_rows):
    cosine, sine = tables(jnp.arange(seq_rows, dtype=jnp.float32))
    half = ROPE // 2
    one = jnp.ones((seq_rows, NOPE), jnp.float32)
    none = jnp.zeros((seq_rows, half), jnp.float32)
    plain = jnp.zeros((seq_rows, NOPE), jnp.float32)
    own = jnp.concatenate([one, cosine, cosine, none, none], axis=1)
    later = jnp.concatenate([plain, -sine, none, none, none], axis=1)
    earlier = jnp.concatenate([plain, none, sine, none, none], axis=1)
    return own, later, earlier


def turn(values, own, later, earlier):
    half = ROPE // 2
    return (
        values * own
        + pltpu.roll(values, LANES - half, 1) * later
        + pltpu.roll(values, half, 1) * earlier
    )


def attention_kernel(
    query_ref, keys_ref, wq_ref, wk_ref, own_ref, later_ref, earlier_ref, shared_ref,
    q_ref, k_ref, kv_ref, out_ref,
):
    seq_rows = query_ref.shape[0]
    heads = wq_ref.shape[1] // LANES
    scale = 1.0 / math.sqrt(NOPE + ROPE)
    lane = lax.broadcasted_iota(jnp.int32, (seq_rows, LANES), 1)
    rows = lax.broadcasted_iota(jnp.int32, (BLOCK, BLOCK), 0)
    cols = lax.broadcasted_iota(jnp.int32, (BLOCK, BLOCK), 1)
    query_raw = jnp.dot(query_ref[...], wq_ref[...], preferred_element_type=jnp.float32)
    keys_raw = jnp.dot(keys_ref[...], wk_ref[...], preferred_element_type=jnp.float32)
    for head in range(heads):
        slot = slice(head * LANES, (head + 1) * LANES)
        q = to_low(turn(query_raw[:, slot], own_ref[...], later_ref[...], earlier_ref[...]))
        kv = to_low(keys_raw[:, slot])
        k = jnp.where(lane < NOPE, kv, shared_ref[...])
        q_ref[:, slot] = q
        k_ref[:, slot] = k
        kv_ref[:, slot] = kv
        for begin in range(0, seq_rows, BLOCK):
            end = begin + BLOCK
            logits = (
                lax.dot_general(
                    q[begin:end], k[:end], (((1,), (1,)), ((), ())),
                    preferred_element_type=jnp.float32,
                )
                * scale
            )
            edge = jnp.where(rows >= cols, logits[:, begin:], -1e30)
            logits = jnp.concatenate([logits[:, :begin], edge], axis=1) if begin else edge
            peak = jnp.max(logits, axis=1, keepdims=True)
            expo = jnp.exp(logits - peak)
            probs = to_low(expo * (1.0 / jnp.sum(expo, axis=1, keepdims=True)))
            found = jnp.dot(probs, kv[:end], preferred_element_type=jnp.float32)
            out_ref[begin:end, head * VDIM : (head + 1) * VDIM] = to_low(found[:, NOPE:])


def attention(query_lat, keys_lat, wq, wk, factors, shared):
    seq_rows = query_lat.shape[0]
    heads = wq.shape[1] // LANES
    whole = pl.BlockSpec(memory_space=pltpu.VMEM)
    wide = jax.ShapeDtypeStruct((seq_rows, heads * LANES), jnp.bfloat16)
    pairs = heads * seq_rows * seq_rows
    return pl.pallas_call(
        attention_kernel,
        in_specs=[whole] * 8,
        out_specs=[whole] * 4,
        out_shape=[wide] * 3 + [jax.ShapeDtypeStruct((seq_rows, heads * VDIM), jnp.bfloat16)],
        compiler_params=pltpu.CompilerParams(vmem_limit_bytes=48 << 20),
        cost_estimate=pl.CostEstimate(
            flops=512 * pairs, bytes_accessed=8 << 20, transcendentals=pairs // 2
        ),
        name="attention",
    )(query_lat, keys_lat, wq, wk, *factors, shared)


def attention_back_kernel(
    q_ref, k_ref, kv_ref, grad_ref, own_ref, later_ref, earlier_ref,
    dq_ref, dkv_ref, shared_ref, key_total, value_total,
):
    seq_rows = q_ref.shape[0]
    heads = q_ref.shape[1] // LANES
    scale = 1.0 / math.sqrt(NOPE + ROPE)
    lane = lax.broadcasted_iota(jnp.int32, (seq_rows, LANES), 1)
    rows = lax.broadcasted_iota(jnp.int32, (BLOCK, BLOCK), 0)
    cols = lax.broadcasted_iota(jnp.int32, (BLOCK, BLOCK), 1)
    for head in range(heads):
        slot = slice(head * LANES, (head + 1) * LANES)
        q, k, kv = q_ref[:, slot], k_ref[:, slot], kv_ref[:, slot]
        grad = grad_ref[:, head * VDIM : (head + 1) * VDIM]
        grad = jnp.concatenate([jnp.zeros_like(grad), grad], axis=1)
        key_total[...] = jnp.zeros_like(key_total)
        value_total[...] = jnp.zeros_like(value_total)
        for begin in range(0, seq_rows, BLOCK):
            end = begin + BLOCK
            q_here, grad_here = q[begin:end], grad[begin:end]
            turned = (((1,), (1,)), ((), ()))
            logits = (
                lax.dot_general(k[:end], q_here, turned, preferred_element_type=jnp.float32)
                * scale
            )
            edge = jnp.where(cols >= rows, logits[begin:], -1e30)
            logits = jnp.concatenate([logits[:begin], edge], axis=0) if begin else edge
            peak = jnp.max(logits, axis=0, keepdims=True)
            expo = jnp.exp(logits - peak)
            probs = expo * (1.0 / jnp.sum(expo, axis=0, keepdims=True))
            grad_probs = lax.dot_general(
                kv[:end], grad_here, turned, preferred_element_type=jnp.float32
            )
            inner = jnp.sum(probs * grad_probs, axis=0, keepdims=True)
            grad_logits = to_low(probs * (grad_probs - inner))
            key_total[:end] += jnp.dot(grad_logits, q_here, preferred_element_type=jnp.float32)
            value_total[:end] += jnp.dot(
                to_low(probs), grad_here, preferred_element_type=jnp.float32
            )
            found = (
                lax.dot_general(
                    grad_logits, k[:end], (((0,), (0,)), ((), ())),
                    preferred_element_type=jnp.float32,
                )
                * scale
            )
            dq_ref[begin:end, slot] = to_low(
                turn(found, own_ref[begin:end], -later_ref[begin:end], -earlier_ref[begin:end])
            )
        keys = key_total[...] * scale
        dkv_ref[:, slot] = to_low(jnp.where(lane < NOPE, keys, value_total[...]))
        if head:
            shared_ref[...] += keys
        else:
            shared_ref[...] = keys


def attention_back(q, k, kv, grad, factors):
    seq_rows, width = q.shape
    whole = pl.BlockSpec(memory_space=pltpu.VMEM)
    wide = jax.ShapeDtypeStruct((seq_rows, width), jnp.bfloat16)
    pairs = width // LANES * seq_rows * seq_rows
    total = pltpu.VMEM((seq_rows, LANES), jnp.float32)
    return pl.pallas_call(
        attention_back_kernel,
        in_specs=[whole] * 7,
        out_specs=[whole] * 3,
        out_shape=[wide, wide, jax.ShapeDtypeStruct((seq_rows, LANES), jnp.float32)],
        scratch_shapes=[total, total],
        compiler_params=pltpu.CompilerParams(vmem_limit_bytes=48 << 20),
        cost_estimate=pl.CostEstimate(
            flops=1280 * pairs, bytes_accessed=10 << 20, transcendentals=pairs // 2
        ),
        name="attention_back",
    )(q, k, kv, grad, *factors)


def to_slots(weight):
    rows = weight.shape[0]
    return jnp.pad(
        weight.reshape(rows, -1, NOPE + ROPE), ((0, 0), (0, 0), (0, LANES - NOPE - ROPE))
    ).reshape(rows, -1)


def from_slots(weight):
    rows = weight.shape[0]
    return weight.reshape(rows, -1, LANES)[:, :, : NOPE + ROPE].reshape(rows, -1)


def pack_rows(block, wide):
    rows, columns = block.shape
    parts = block.reshape(rows // 16, 16, columns)
    parts = jnp.pad(parts, ((0, 0), (0, 0), (0, wide - columns)))
    return parts.transpose(1, 0, 2).reshape(16, -1)


def unpack_rows(packed, wide, columns):
    count = packed.shape[2] // wide
    parts = packed.reshape(packed.shape[0], 16, count, wide)[..., :columns]
    return parts.transpose(0, 2, 1, 3).reshape(packed.shape[0], -1, columns)


def shards(
    block_input,
    out_grad,
    norm_gains,
    latent_weight,
    query_weight,
    keys_weight,
    output_weight,
    gate_weight,
    up_weight,
    down_weight,
    gains_moment,
    gains_second,
    latent_moment,
    latent_second,
    query_moment,
    query_second,
    keys_moment,
    keys_second,
    output_moment,
    output_second,
    gate_moment,
    gate_second,
    up_moment,
    up_second,
    down_moment,
    down_second,
):
    place = {name: lax.axis_index(name) for name in AXES}
    place["y"] = place["yh"] * 2 + place["yl"]
    group_index = place["c"] * RING + place["z"]
    tok_rows = block_input.shape[0]
    seq_rows = tok_rows * 2 * RING
    heads_here = output_weight.shape[0] // VDIM
    width = QR + KVR + ROPE
    gain_width = norm_gains.shape[0]

    latent_rows = latent_weight.shape[0]
    latent_pad = 24 - latent_rows
    gain_row = jnp.pad(to_low(norm_gains)[None], ((0, latent_pad - 1), (0, width - gain_width)))
    latent_block = jnp.concatenate([to_low(latent_weight), gain_row], axis=0)
    latent_mine = lax.all_to_all(
        jnp.broadcast_to(latent_block[None], (64,) + latent_block.shape),
        PLANE + ("z",),
        split_axis=0,
        concat_axis=0,
        tiled=True,
    )
    wide = heads_here * LANES
    key_cols = keys_weight.shape[1]
    small = swap(
        jnp.concatenate(
            [
                pack_rows(to_slots(to_low(query_weight)), wide),
                to_low(keys_weight),
                pack_rows(to_low(output_weight).T, 384),
            ],
            axis=1,
        )
    )
    tokens = swap(block_input).astype(jnp.float32)
    hidden_here = gate_weight.shape[1]
    fill = -hidden_here % LANES
    both = mix(
        *[jnp.pad(to_low(weight), ((0, 0), (0, fill))) for weight in (gate_weight, up_weight)]
    )
    cut = both.shape[1] - CELL
    weights_one = both[:, :cut]
    weights_two = jnp.pad(to_low(down_weight).T, ((0, 0), (0, fill)))
    weights_two = jnp.concatenate([both[:, cut:], weights_two], axis=1)
    own_pos = (group_index * tok_rows + jnp.arange(tok_rows)).astype(jnp.float32)
    own_cos, own_sin = tables(own_pos)
    factor_one = lax.rsqrt(jnp.mean(tokens * tokens, axis=-1, keepdims=True) + EPS)
    spaced = tokens * factor_one
    spaced = jnp.pad(
        spaced.reshape(tok_rows, 8, 2, 8, latent_rows),
        ((0, 0), (0, 0), (0, 0), (0, 0), (0, latent_pad)),
    )
    core_first = place["c"] == 0
    spaced_mine = jnp.where(core_first, spaced[:, :, 0], spaced[:, :, 1]).reshape(tok_rows, -1)
    spaced_other = jnp.where(core_first, spaced[:, :, 1], spaced[:, :, 0]).reshape(tok_rows, -1)
    small = jnp.broadcast_to(small[None], (16,) + small.shape)
    latent_mine, spaced_mine, spaced_other, small = tie(
        [latent_mine, spaced_mine, spaced_other, small], weights_one, weights_two
    )
    latent_other = send_core(latent_mine)
    small = exchange_plane(small)

    def in_cores(mine, other, extra):
        first = jnp.where(core_first, mine, other).reshape((8, 8) + extra)
        second = jnp.where(core_first, other, mine).reshape((8, 8) + extra)
        return jnp.stack([first, second], axis=1)

    gains_all = in_cores(
        latent_mine[:, latent_rows, :gain_width],
        latent_other[:, latent_rows, :gain_width],
        (gain_width,),
    )
    gains_all = gains_all.astype(jnp.float32).reshape(-1)
    gain_one = gains_all[:D]
    gain_two = gains_all[D : 2 * D]
    gain_query = gains_all[2 * D : 2 * D + QR]
    gain_keys = gains_all[2 * D + QR :]
    latent_full = in_cores(
        latent_mine[:, :latent_rows], latent_other[:, :latent_rows], (latent_rows, width)
    ).reshape(-1, width)

    normed = to_low(tokens * factor_one * gain_one)
    spaced_gain = jnp.pad(
        gain_one.reshape(8, 2, 8, latent_rows), ((0, 0), (0, 0), (0, 0), (0, latent_pad))
    )
    gain_mine = jnp.where(core_first, spaced_gain[:, 0], spaced_gain[:, 1]).reshape(-1)
    gain_other = jnp.where(core_first, spaced_gain[:, 1], spaced_gain[:, 0]).reshape(-1)
    latent = jnp.dot(
        to_low(spaced_mine * gain_mine),
        latent_mine.reshape(-1, width),
        preferred_element_type=jnp.float32,
    ) + jnp.dot(
        to_low(spaced_other * gain_other),
        latent_other.reshape(-1, width),
        preferred_element_type=jnp.float32,
    )
    query_part = latent[:, :QR]
    keys_part = latent[:, QR : QR + KVR]
    query_pre, factor_query = rms_forward(query_part, gain_query)
    keys_pre, factor_keys = rms_forward(keys_part, gain_keys)
    packed = jnp.concatenate(
        [
            to_low(query_pre),
            to_low(keys_pre),
            to_low(rotate(latent[:, QR + KVR :], own_cos, own_sin)),
        ],
        axis=1,
    )
    packed_pairs = gather_group(packed)
    gathered = to_abs([p[0] for p in packed_pairs], [p[1] for p in packed_pairs], place)
    gathered, small, weights_one, weights_two, out_grad = tie(
        [gathered, small, weights_one, weights_two, out_grad]
    )
    line_one = by_four(four_copies(trade(weights_one, True)), "x")
    line_two = first_y(trade(weights_two, False), place)
    cotangent = swap(out_grad).astype(jnp.float32)
    cot_block = to_low(RESIDUAL * cotangent)
    cot_all = joined(gather_group(cot_block))
    query_full = unpack_rows(small[:, :, : 3 * wide], wide, wide).reshape(-1, wide)
    keys_matrix = small[:, :, 3 * wide : 3 * wide + key_cols].reshape(-1, key_cols)
    output_turned = unpack_rows(small[:, :, 3 * wide + key_cols :], 384, SLICE).reshape(-1, SLICE)
    query_lat = gathered[:, :QR]
    keys_lat = gathered[:, QR : QR + KVR]
    shared_rot = gathered[:, QR + KVR :]
    factors = rope_slots(seq_rows)
    shared_slot = jnp.pad(shared_rot, ((0, 0), (NOPE, LANES - NOPE - ROPE)))
    query_lat, line_one, line_two = tie([query_lat, line_one, line_two])
    queries, keys_all, keys_values, attended = attention(
        query_lat, keys_lat, query_full, keys_matrix, factors, shared_slot
    )
    attended_mine, attended_other = to_rel(attended, place)

    def to_model(rows):
        return to_low(
            jnp.einsum("sa,da->sd", rows, output_turned, preferred_element_type=jnp.float32)
        )

    branch_sums = halves_sums(to_model(attended_mine), to_model(attended_other))
    down, up = ring_across(branch_sums)
    weights_one = by_four(four_copies(line_one), ("yl", "yh")).reshape(D, -1)
    weights_two = second_x(line_two, place).reshape(D, -1)
    down_turned = weights_two[:, CELL:]
    branch = ring_finish(branch_sums, down, up)
    hidden_state = tokens + RESIDUAL * branch
    mlp_pre, factor_two = rms_forward(hidden_state, gain_two)

    mlp_pairs = gather_group(to_low(mlp_pre))
    grad_hidden = jnp.dot(cot_all, down_turned, preferred_element_type=jnp.float32)
    grad_hidden, latent_full = tie([grad_hidden, latent_full])
    held, back_pairs = (), []
    for spot in (0, 1):
        near, far = mlp_pairs[2 * spot : 2 * spot + 2]
        *backs, rows, hidden, both = feed_forward(
            near + far, grad_hidden, weights_one, weights_two, held, spot
        )
        held = (rows, hidden, both)
        back_pairs += [backs[:2], backs[2:]]
    mlp_all, hidden_all, grad_both = held
    grad_mlp_in = scatter_group(back_pairs)
    grad_one = to_low(
        jnp.einsum("sd,sf->df", mlp_all, grad_both[:, :cut], preferred_element_type=jnp.float32)
    )
    grad_two = jnp.concatenate(
        [
            to_low(jnp.einsum("sd,sf->df", rows, part, preferred_element_type=jnp.float32))
            for rows, part in ((mlp_all, grad_both[:, cut:]), (cot_all, hidden_all))
        ],
        axis=1,
    )
    terms_one = by_four(grad_one.reshape(RING, -1, cut), ("yl", "yh"))
    fold_two = fold_x(grad_two.reshape(RING, -1, grad_two.shape[1]), place)

    grad_norm_two, grad_gain_two = rms_backward(grad_mlp_in, hidden_state, factor_two, gain_two)
    grad_state = cotangent + grad_norm_two
    branch_all = joined(gather_group(to_low(RESIDUAL * grad_state)))
    mlp_terms = [
        to_low(
            jnp.einsum(
                "sf,df->sd",
                hidden_all.reshape(RING, 2, tok_rows, -1)[:, index].reshape(RING * tok_rows, -1),
                down_turned,
                preferred_element_type=jnp.float32,
            )
        )
        for index in (0, 1)
    ]
    branch_all, *mlp_terms = tie([branch_all] + mlp_terms)
    attended_pairs = jnp.stack(
        [attended_mine.reshape(RING, tok_rows, -1), attended_other.reshape(RING, tok_rows, -1)],
        axis=1,
    ).reshape(seq_rows, -1)
    grad_output = to_low(
        jnp.einsum("sd,sa->da", branch_all, attended_pairs, preferred_element_type=jnp.float32)
    )
    grad_parts = to_low(
        jnp.dot(branch_all, output_turned, preferred_element_type=jnp.float32)
    ).reshape(RING, 2, tok_rows, -1)
    grad_attended = to_abs(
        [grad_parts[step, 0] for step in range(RING)],
        [grad_parts[step, 1] for step in range(RING)],
        place,
    )
    block_output = hidden_state + RESIDUAL * scatter_halves(*mlp_terms)
    grad_attended, normed = tie([grad_attended, normed])
    normed_cols = normed.reshape(tok_rows, 2 * RING, SLICE).transpose(1, 0, 2)
    normed_parts = []
    for step in range(RING):
        spot = (place["z"] + step) % RING
        pair = jnp.stack(
            [
                lax.dynamic_index_in_dim(normed_cols, core * RING + spot, axis=0, keepdims=False)
                for core in (place["c"], 1 - place["c"])
            ]
        )
        normed_parts.append(send_z(pair, step) if step else pair)
    normed_parts = jnp.stack(normed_parts)
    normed_all = jnp.stack([normed_parts[:, 0], send_core(normed_parts[:, 1])], axis=1)
    normed_all = normed_all.reshape(seq_rows, SLICE)
    grad_query_raw, grad_keys_raw, grad_shared = attention_back(
        queries, keys_all, keys_values, grad_attended, factors
    )
    grad_shared = grad_shared[:, NOPE : NOPE + ROPE]
    grad_query_w = to_low(
        jnp.einsum("sr,sc->rc", query_lat, grad_query_raw, preferred_element_type=jnp.float32)
    )
    grad_keys_w = to_low(
        jnp.einsum("sr,sc->rc", keys_lat, grad_keys_raw, preferred_element_type=jnp.float32)
    )
    small_grads = jnp.concatenate(
        [
            jax.vmap(lambda block: pack_rows(block, wide))(grad_query_w.reshape(16, -1, wide)),
            grad_keys_w.reshape(16, 16, key_cols),
            jax.vmap(lambda block: pack_rows(block, 384))(grad_output.reshape(16, -1, SLICE)),
        ],
        axis=2,
    )
    latent_terms = to_low(
        jnp.concatenate(
            [
                jnp.einsum(
                    "sc,rc->sr", grad_query_raw, query_full, preferred_element_type=jnp.float32
                ),
                jnp.einsum(
                    "sc,rc->sr", grad_keys_raw, keys_matrix, preferred_element_type=jnp.float32
                ),
                grad_shared,
            ],
            axis=1,
        )
    )
    latent_terms, block_output, small_grads, terms_one = tie(
        [latent_terms, block_output, small_grads, terms_one]
    )
    terms_one = by_four(add_up(terms_one).reshape(RING, -1, cut), "x")
    grad_latent_in = scatter_halves(*to_rel(latent_terms, place))
    grad_latent_in, small_grads, terms_one, fold_two = tie(
        [grad_latent_in, small_grads, terms_one, fold_two]
    )
    small_terms = exchange_plane(small_grads)
    sum_one = trade_back(add_up(terms_one), True)
    sum_two = trade_back(fold_y(fold_two.reshape(RING, -1, fold_two.shape[1]), place), False)
    grad_query_pre, grad_gain_query = rms_backward(
        grad_latent_in[:, :QR], query_part, factor_query, gain_query
    )
    grad_keys_pre, grad_gain_keys = rms_backward(
        grad_latent_in[:, QR : QR + KVR], keys_part, factor_keys, gain_keys
    )
    grad_rope = unrotate(grad_latent_in[:, QR + KVR :], own_cos, own_sin)
    grad_latent = to_low(jnp.concatenate([grad_query_pre, grad_keys_pre, grad_rope], axis=1))
    grad_normed = jnp.einsum(
        "sc,dc->sd", grad_latent, latent_full, preferred_element_type=jnp.float32
    )
    grad_norm_one, grad_gain_one = rms_backward(grad_normed, tokens, factor_one, gain_one)
    input_grad = swap(to_low(grad_state + grad_norm_one)).astype(jnp.float32)

    latent_grads = joined(gather_group(grad_latent))
    latent_grads, block_output = tie([latent_grads, block_output])
    block_output = swap(to_low(block_output)).astype(jnp.float32)
    grad_latent_w = jnp.einsum(
        "sd,sc->dc",
        normed_all,
        latent_grads,
        preferred_element_type=jnp.float32,
    )
    grad_gains = jnp.concatenate(
        [grad_gain_one, grad_gain_two, grad_gain_query, grad_gain_keys]
    ).reshape(2, RING, -1)
    gains_line = lax.dynamic_index_in_dim(grad_gains, place["c"], axis=0, keepdims=False)
    gains_line = gains_line + send_core(
        lax.dynamic_index_in_dim(grad_gains, 1 - place["c"], axis=0, keepdims=False)
    )


    def gains_at(step):
        spot = (place["z"] + step) % RING
        return lax.dynamic_index_in_dim(gains_line, spot, axis=0, keepdims=True)

    gains_sum = gains_at(0)
    for step in (1, 2, 3):
        gains_sum = gains_sum + send_z(gains_at(step), step)
    gains_rows = jnp.pad(gains_sum.reshape(16, 1, gain_width), ((0, 0), (0, 0), (0, width - gain_width)))
    last = to_low(jnp.concatenate([grad_latent_w.reshape(16, -1, width), gains_rows], axis=1))
    last, small_terms, sum_one, sum_two = tie([last, small_terms, sum_one, sum_two])
    sum_down = sum_two[:, CELL : CELL + hidden_here].astype(jnp.float32).T
    sum_gate, sum_up = (
        part[:, :hidden_here].astype(jnp.float32)
        for part in unmix(jnp.concatenate([sum_one, sum_two[:, :CELL]], axis=1))
    )
    sum_small = swap(add_up(small_terms)).astype(jnp.float32)
    sum_query = from_slots(unpack_rows(sum_small[None, :, : 3 * wide], wide, wide)[0])
    sum_keys = sum_small[:, 3 * wide : 3 * wide + key_cols]
    sum_output = unpack_rows(sum_small[None, :, 3 * wide + key_cols :], 384, SLICE)[0].T
    last = scatter_plane(last)
    route = []
    for source in range(128):
        rest, at_z = divmod(source, 4)
        rest, at_yh = divmod(rest, 2)
        rest, at_c = divmod(rest, 2)
        at_yl, at_x = divmod(rest, 4)
        route.append((source, 16 * (at_c * 4 + at_z) + (at_yl * 4 + at_x) * 2 + at_yh))
    last = lax.ppermute(last, AXES, route).astype(jnp.float32)
    sum_latent = last[:-1]
    sum_gains = last[-1, :gain_width]

    rates = rate_table()
    next_gains, moment_gains, second_gains = adamw(
        norm_gains, sum_gains, gains_moment, gains_second, rates[0], 0.0
    )
    next_latent, moment_latent, second_latent = adamw(
        latent_weight, sum_latent, latent_moment, latent_second, rates[1], 0.1
    )
    next_query, moment_query, second_query = adamw(
        query_weight, sum_query, query_moment, query_second, rates[2], 0.1
    )
    next_keys, moment_keys, second_keys = adamw(
        keys_weight, sum_keys, keys_moment, keys_second, rates[3], 0.1
    )
    next_output, moment_output, second_output = adamw(
        output_weight, sum_output, output_moment, output_second, rates[4], 0.1
    )
    next_gate, moment_gate, second_gate = adamw(
        gate_weight, sum_gate, gate_moment, gate_second, rates[5], 0.1
    )
    next_up, moment_up, second_up = adamw(
        up_weight, sum_up, up_moment, up_second, rates[6], 0.1
    )
    next_down, moment_down, second_down = adamw(
        down_weight, sum_down, down_moment, down_second, rates[7], 0.1
    )
    return (
        block_output,
        input_grad,
        next_gains,
        moment_gains,
        second_gains,
        next_latent,
        moment_latent,
        second_latent,
        next_query,
        moment_query,
        second_query,
        next_keys,
        moment_keys,
        second_keys,
        next_output,
        moment_output,
        second_output,
        next_gate,
        moment_gate,
        second_gate,
        next_up,
        moment_up,
        second_up,
        next_down,
        moment_down,
        second_down,
    )


def solution(mesh):
    devices = jax.sharding.Mesh(mesh.devices.reshape(SIZES), AXES)
    rows, split = ("yl", "x", "c"), ("yh", "z")
    whole = rows + split
    tokens, flat = P(whole, None), P(whole)
    by_rows, by_cols = P(rows, split), P(split, rows)
    weights = (flat, tokens, by_rows, by_rows, by_cols, by_rows, by_rows, by_cols)
    return jax.shard_map(
        shards,
        mesh=devices,
        in_specs=(tokens, tokens) + weights + tuple(s for s in weights for _ in range(2)),
        out_specs=(tokens, tokens) + tuple(s for s in weights for _ in range(3)),
        check_vma=False,
    )
```
